32 devices in a mesh: seg: 8 (over z, core), section: 4 (over y, x).
Axes of the slice: x: 2, y: 2, z: 4, core: 2. Of those that a mesh axis runs over, the one named last changes fastest.
Arguments:
- leaving: bfloat16 [8, 4, 272, 4096], P('seg', 'section'), may hold values from -6 to 6
- w_query: bfloat16 [4, 4096, 2048], P('section'), may hold values from -0.09375 to 0.09375
- w_key: bfloat16 [4, 4096, 2048], P('section', None, 'seg'), may hold values from -0.09375 to 0.09375
- w_value: bfloat16 [4, 4096, 4096], P('section', None, 'seg'), may hold values from -0.09375 to 0.09375
- w_gate: bfloat16 [4, 4096], P('section'), may hold values from -0.09375 to 0.09375
- norm_gain: bfloat16 [4, 4096], P('section'), may hold values from 0.5 to 1.5
- memory_matrix: bfloat16 [4, 4096, 2048], P('section', 'seg'), may hold values from -24 to 24
- key_totals: float32 [4, 2048], P('section'), may hold values from 0.02 to 0.5
- doc_starts: int32 [4, 8], P('section'), may hold values 0 or 1
Outputs:
- updated: bfloat16 [8, 4, 272, 4096], P('seg', 'section')
- matrix_next: bfloat16 [4, 4096, 2048], P('section', 'seg')
- totals_next: float32 [4, 2048], P('section')
The draws below stay inside these ranges and needn't reach their ends.
All inputs are finite; a program needn't handle non-finite values. No bound on the sum of `doc_starts` on one device may be relied on, other than what follows from the above.
Results may differ from the reference program's by a relative error of at most 0.01.
Values may be sent and summed in bfloat16 or wider, within the bound.
A program may use at most 128 MiB of HBM per device.

```python
import math
import jax
import jax.numpy as jnp
from jax import lax

D = 4096
DK = 2048
MEM = 16
ROWS = 272
SEGS = 8
SECTIONS = 4


def set_ends(entries, own_key, low, top_value):
    longest = entries.shape.index(max(entries.shape))
    spots = []
    for shift in (0, 1):
        where = [jax.random.randint(jax.random.fold_in(own_key, axis), (), 0, length) for axis, length in enumerate(entries.shape)]
        where[longest] = (where[longest] + shift) % entries.shape[longest]
        spots.append(tuple(where))
    return entries.at[spots[0]].set(low).at[spots[1]].set(top_value)


def block_levels(stream_key, shape, pieces, smallest, top_value):
    def one(position, blocks):
        steps = jax.random.uniform(jax.random.fold_in(jax.random.fold_in(stream_key, 6), position), (blocks,), jnp.float32, smallest / len(pieces), top_value / len(pieces))
        return jnp.repeat(jnp.exp(steps), shape[position] // blocks).reshape((-1,) + (1,) * (len(shape) - position - 1))

    factor_of = one(*pieces[0])
    for cut in pieces[1:]:
        factor_of = factor_of * one(*cut)
    return factor_of


def gaussian(stream_key, shape, width, reach, pieces=(), kind=jnp.bfloat16):
    result = jax.random.normal(stream_key, shape, jnp.float32) * width
    if len(pieces) > 0:
        result = block_levels(stream_key, shape, pieces, -0.22, 0.18) * result
    return jnp.clip(result, min=-reach, max=reach).astype(kind)


def setup_inputs(seed: int = 0) -> dict:
    key_list = jax.random.split(jax.random.key(seed), 10)
    leaving = gaussian(key_list[0], (SEGS, SECTIONS, ROWS, D), 1.0, 6.0, ((0, 8), (1, 4)))
    w_query = gaussian(key_list[1], (SECTIONS, D, DK), D ** -0.5, 0.09375, ((0, 4),))
    w_key = gaussian(key_list[2], (SECTIONS, D, DK), D ** -0.5, 0.09375, ((0, 4), (2, 8)))
    w_value = gaussian(key_list[3], (SECTIONS, D, D), D ** -0.5, 0.09375, ((0, 4), (2, 8)))
    w_gate = gaussian(key_list[4], (SECTIONS, D), D ** -0.5, 0.09375, ((0, 4),))
    norm_gain = jnp.clip(1.0 + 0.1 * jax.random.normal(key_list[5], (SECTIONS, D), jnp.float32), 0.5, 1.5).astype(jnp.bfloat16)
    memory_matrix = gaussian(key_list[6], (SECTIONS, D, DK), 4.0, 24.0, ((0, 4), (1, 8)))
    key_totals = jnp.clip(jnp.exp(math.log(0.5) - 3.218876 * jax.random.uniform(key_list[7], (SECTIONS, DK), jnp.float32) ** block_levels(key_list[7], (SECTIONS, DK), ((0, 4),), -0.2, 0.2)), 0.02, 0.5)
    doc_starts = set_ends((jax.random.randint(key_list[8], (SECTIONS, SEGS), 0, 8) < 1).astype(jnp.int32), jax.random.fold_in(key_list[8], 1), 0, 1)
    return {"leaving": leaving, "w_query": w_query, "w_key": w_key, "w_value": w_value, "w_gate": w_gate, "norm_gain": norm_gain, "memory_matrix": memory_matrix, "key_totals": key_totals, "doc_starts": doc_starts}


highest = lax.Precision.HIGHEST
epsilon = 1e-05

def feature_map(projected):
    return jax.nn.elu(projected) + 1.0

def visibility(starts_row):
    seg_total = starts_row.shape[0]
    positions = jnp.arange(seg_total, dtype=jnp.int32)
    last_start = lax.cummax(jnp.where(starts_row == 1, positions, jnp.int32(-1)), axis=0)
    fresh_flag = (last_start < 0).astype(jnp.float32)
    seen_pairs = ((positions[:, None] >= last_start[None, :]) & (positions[:, None] < positions[None, :])).astype(jnp.float32)
    seen_final = (positions >= last_start[seg_total - 1]).astype(jnp.float32)
    return (fresh_flag, seen_pairs, seen_final)

def one_section(entering, query_proj, key_proj, value_proj, gate_vector, gain_row, matrix, totals_base, starts_row):
    seg_count = entering.shape[0]
    row_count = entering.shape[1]
    feature_count = entering.shape[2]
    wide_rows = entering.astype(jnp.float32)
    inverse_rms = lax.rsqrt(lax.optimization_barrier(jnp.mean(wide_rows * wide_rows, axis=-1, keepdims=True)) + epsilon)
    normed = (wide_rows * inverse_rms * gain_row.astype(jnp.float32)).astype(jnp.bfloat16)
    flat_rows = normed.reshape(seg_count * row_count, feature_count)
    queries = feature_map(jnp.dot(flat_rows, query_proj, preferred_element_type=jnp.float32)).astype(jnp.bfloat16)
    memory = normed[:, :MEM, :].reshape(seg_count * MEM, feature_count)
    key_rows = feature_map(jnp.dot(memory, key_proj, preferred_element_type=jnp.float32)).astype(jnp.bfloat16)
    values = jnp.dot(memory, value_proj, preferred_element_type=jnp.float32)
    gate_rates = jax.nn.sigmoid(jnp.dot(memory, gate_vector, preferred_element_type=jnp.float32))
    fresh_flag, seen_pairs, seen_final = visibility(starts_row)
    key_wide = key_rows.astype(jnp.float32)
    key_sums = key_wide.reshape(seg_count, MEM, -1).sum(axis=1)
    totals = fresh_flag[:, None] * totals_base[None, :] + jnp.dot(seen_pairs.T, key_sums, precision=highest)
    total_rows = jnp.repeat(totals, MEM, axis=0)
    key_scales = jnp.maximum(lax.optimization_barrier(jnp.sum(total_rows * key_wide, axis=-1)), 1.0)
    fresh_rows = jnp.repeat(fresh_flag, MEM)
    key_gram = jnp.dot(key_rows, key_rows.T, preferred_element_type=jnp.float32)
    probed_keys = jnp.dot(key_rows, matrix.T, preferred_element_type=jnp.float32)
    initial = gate_rates[:, None] * (values - fresh_rows[:, None] * probed_keys / key_scales[:, None])
    seen_cols = jnp.repeat(jnp.repeat(seen_pairs, MEM, axis=0), MEM, axis=1)
    mixing = seen_cols * key_gram * (gate_rates / key_scales)[None, :]
    writes = jnp.zeros_like(values)
    for segment in range(seg_count):
        mix_cols = mixing[:, segment * MEM:(segment + 1) * MEM]
        candidate = initial[segment * MEM:(segment + 1) * MEM] - jnp.dot(mix_cols.T, writes, precision=highest)
        writes = writes.at[segment * MEM:(segment + 1) * MEM].set(candidate)
    base_read = jnp.dot(queries, matrix.T, preferred_element_type=jnp.float32)
    column_mask = jnp.repeat(jnp.repeat(seen_pairs.T, row_count, axis=0), MEM, axis=1)
    similarity = jnp.dot(queries, key_rows.T, preferred_element_type=jnp.float32) * column_mask
    low_rank = jnp.dot(similarity, writes, precision=highest)
    query_totals = jnp.repeat(totals, row_count, axis=0)
    denominator = jnp.maximum(lax.optimization_barrier(jnp.sum(queries.astype(jnp.float32) * query_totals, axis=-1)), 1.0)
    fresh_query = jnp.repeat(fresh_flag, row_count)
    updated = (wide_rows.reshape(seg_count * row_count, feature_count) + (fresh_query[:, None] * base_read + low_rank) / denominator[:, None]).astype(jnp.bfloat16)
    updated = updated.reshape(seg_count, row_count, feature_count)
    fresh_end = fresh_flag[seg_count - 1]
    end_rows = jnp.repeat(seen_final, MEM)
    matrix_next = (fresh_end * matrix.astype(jnp.float32) + jnp.dot((writes * end_rows[:, None]).T, key_wide, precision=highest)).astype(jnp.bfloat16)
    totals_next = fresh_end * totals_base + jnp.dot(seen_final, key_sums, precision=highest)
    return (updated, matrix_next, totals_next)

def reference(leaving, w_query, w_key, w_value, w_gate, norm_gain, memory_matrix, key_totals, doc_starts):
    entering = jnp.moveaxis(jnp.roll(leaving, 1, axis=1), 1, 0)

    def section_work(packed):
        return one_section(*packed)
    updated, matrix_next, totals_next = lax.map(section_work, (entering, w_query, w_key, w_value, w_gate, norm_gain, memory_matrix, key_totals, doc_starts))
    return (jnp.moveaxis(updated, 0, 1), matrix_next, totals_next)
```

```python
import jax
import jax.numpy as jnp
from jax import lax
from jax.sharding import PartitionSpec as P

MEM = 16


highest = lax.Precision.HIGHEST
epsilon = 1e-05


def shifted(shard, axis, by):
    size = lax.axis_size(axis)
    return lax.ppermute(shard, axis, [(i, (i + by) % size) for i in range(size)])


def feature_map(projected):
    return jax.nn.elu(projected) + 1.0


def contract_last(left_rows, right_rows):
    return lax.dot_general(
        left_rows, right_rows, (((1,), (1,)), ((), ())), preferred_element_type=jnp.float32
    )


def contract_first(left_rows, right_rows):
    return lax.dot_general(
        left_rows,
        right_rows,
        (((0,), (0,)), ((), ())),
        precision=highest,
        preferred_element_type=jnp.float32,
    )


def visibility(starts_row):
    seg_total = starts_row.shape[0]
    positions = jnp.arange(seg_total, dtype=jnp.int32)
    last_start = lax.cummax(jnp.where(starts_row == 1, positions, jnp.int32(-1)), axis=0)
    fresh_flag = (last_start < 0).astype(jnp.float32)
    seen_pairs = (
        (positions[:, None] >= last_start[None, :]) & (positions[:, None] < positions[None, :])
    ).astype(jnp.float32)
    seen_final = (positions >= last_start[seg_total - 1]).astype(jnp.float32)
    return (fresh_flag, seen_pairs, seen_final)


def normalized(rows, gain_row):
    wide = rows.astype(jnp.float32)
    inverse_rms = lax.rsqrt(jnp.mean(wide * wide, axis=-1, keepdims=True) + epsilon)
    return (wide * inverse_rms * gain_row.astype(jnp.float32)).astype(jnp.bfloat16)


def solved(mixing, initial):
    size = mixing.shape[0]
    power = -mixing.T
    writes = initial + jnp.dot(power, initial, precision=highest)
    span = 2
    while span < size // MEM:
        power = jnp.dot(power, power, precision=highest)
        writes = writes + jnp.dot(power, writes, precision=highest)
        span *= 2
    return writes


def chain_start(matrix):
    cores = (0, 1)
    inward = [(c, 2 + c) for c in cores] + [(6 + c, 4 + c) for c in cores]
    across = [(2 + c, 4 + c) for c in cores] + [(4 + c, 2 + c) for c in cores]
    from_middle = lax.ppermute(matrix, "seg", across)
    from_outer = lax.ppermute(matrix, "seg", inward)
    from_far = lax.ppermute(from_outer, "seg", across)
    return (matrix, from_outer, from_middle, from_far)


def chain_read(slices, queries):
    cores = (0, 1)
    inward = [(c, 2 + c) for c in cores] + [(6 + c, 4 + c) for c in cores]
    outward = [(b, a) for a, b in inward]
    outward_crossed = [(b, a ^ 1) for a, b in inward]
    swap = [(i, i ^ 1) for i in range(8)]
    rows = queries.shape[0]
    my_index = lax.axis_index("seg")
    core = my_index % 2
    low_half = my_index < 4
    is_outer = (my_index < 2) | (my_index >= 6)
    own, from_outer, from_middle, from_far = slices
    guests = lax.ppermute(queries, "seg", inward)
    chip_rows = jnp.concatenate([queries, lax.ppermute(queries, "seg", swap)], axis=0)
    guest_rows = jnp.concatenate([guests, lax.ppermute(guests, "seg", swap)], axis=0)

    def read(some_rows, piece):
        return contract_last(some_rows, piece).astype(jnp.bfloat16)

    def spread(chip_part, guest_part):
        mine = (chip_part[:rows], lax.ppermute(chip_part[rows:], "seg", swap))
        if guest_part is None:
            return mine, None
        back = (
            lax.ppermute(guest_part[:rows], "seg", outward),
            lax.ppermute(guest_part[rows:], "seg", outward_crossed),
        )
        return mine, back

    own_mine, own_back = spread(read(chip_rows, own), read(guest_rows, own))
    outer_mine, _ = spread(read(chip_rows, from_outer), None)
    both = jnp.concatenate([chip_rows, guest_rows], axis=0)
    middle = read(both, from_middle)
    middle_mine, middle_back = spread(middle[: 2 * rows], middle[2 * rows :])
    far = read(both, from_far)
    far_mine, far_back = spread(far[: 2 * rows], far[2 * rows :])

    def pick(when_outer, when_inner):
        chosen = [jnp.where(is_outer, a, b) for a, b in zip(when_outer, when_inner)]
        first = jnp.where(core == 0, chosen[0], chosen[1])
        second = jnp.where(core == 0, chosen[1], chosen[0])
        return jnp.concatenate([first, second], axis=1)

    ordered = [
        pick(own_mine, outer_mine),
        pick(own_back, own_mine),
        pick(middle_back, middle_mine),
        pick(far_back, far_mine),
    ]
    return jnp.concatenate(
        [jnp.where(low_half, ordered[k], ordered[3 - k]) for k in range(4)], axis=1
    ).astype(jnp.float32)


def local(
    leaving, w_query, w_key, w_value, w_gate, norm_gain, memory_matrix, key_totals, doc_starts
):
    seg_count = lax.axis_size("seg")
    my_index = lax.axis_index("seg")
    memory_rows = shifted(leaving[0, 0, :MEM], "section", 1)
    entering = shifted(leaving, "section", 1)[0, 0]
    matrix = memory_matrix[0]
    chained = seg_count == 8
    if chained:
        slices = chain_start(matrix)
    else:
        whole_matrix = lax.all_gather(matrix, "seg", axis=0, tiled=True)
    memory = lax.all_gather(normalized(memory_rows, norm_gain[0]), "seg", axis=0, tiled=True)
    key_part = feature_map(jnp.dot(memory, w_key[0], preferred_element_type=jnp.float32)).astype(
        jnp.bfloat16
    )
    value_part = jnp.dot(memory, w_value[0], preferred_element_type=jnp.float32)
    gate_rates = jax.nn.sigmoid(jnp.dot(memory, w_gate[0], preferred_element_type=jnp.float32))
    key_rows = lax.all_gather(key_part, "seg", axis=1, tiled=True)
    fresh_flag, seen_pairs, seen_final = visibility(doc_starts[0])
    key_wide = key_rows.astype(jnp.float32)
    key_sums = key_wide.reshape(seg_count, MEM, -1).sum(axis=1)
    totals = fresh_flag[:, None] * key_totals[0][None, :] + jnp.dot(
        seen_pairs.T, key_sums, precision=highest
    )
    total_rows = jnp.repeat(totals, MEM, axis=0)
    key_scales = jnp.maximum(jnp.sum(total_rows * key_wide, axis=-1), 1.0)
    key_gram = contract_last(key_rows, key_rows)
    seen_cols = jnp.repeat(jnp.repeat(seen_pairs, MEM, axis=0), MEM, axis=1)
    mixing = seen_cols * key_gram * (gate_rates / key_scales)[None, :]
    fresh_rows = jnp.repeat(fresh_flag, MEM)
    probed_keys = contract_last(key_rows, matrix)
    initial = gate_rates[:, None] * (
        value_part - (fresh_rows / key_scales)[:, None] * probed_keys
    )
    write_cols = solved(mixing, initial)
    writes = lax.all_gather(write_cols.astype(jnp.bfloat16), "seg", axis=1, tiled=True)
    fresh_end = fresh_flag[seg_count - 1]
    end_rows = jnp.repeat(seen_final, MEM)
    matrix_next = (
        fresh_end * matrix.astype(jnp.float32)
        + contract_first(write_cols * end_rows[:, None], key_wide)
    ).astype(jnp.bfloat16)
    totals_next = fresh_end * key_totals[0] + jnp.dot(seen_final, key_sums, precision=highest)
    normed = normalized(entering, norm_gain[0])
    queries = feature_map(jnp.dot(normed, w_query[0], preferred_element_type=jnp.float32)).astype(
        jnp.bfloat16
    )
    my_fresh = fresh_flag[my_index]
    column_mask = jnp.repeat(seen_pairs[:, my_index], MEM)
    my_totals = lax.dynamic_slice_in_dim(totals, my_index, 1, 0)
    denominator = jnp.maximum(jnp.sum(queries.astype(jnp.float32) * my_totals, axis=-1), 1.0)
    similarity = contract_last(queries, key_rows) * column_mask[None, :]
    low_rank = jnp.dot(
        similarity.astype(jnp.bfloat16), writes, preferred_element_type=jnp.float32
    )
    if chained:
        base_read = chain_read(slices, queries)
    else:
        base_read = contract_last(queries, whole_matrix)
    updated = (
        entering.astype(jnp.float32) + (my_fresh * base_read + low_rank) / denominator[:, None]
    ).astype(jnp.bfloat16)
    return (updated[None, None], matrix_next[None], totals_next[None])


def solution(mesh):
    return jax.shard_map(
        local,
        mesh=mesh,
        in_specs=(
            P("seg", "section", None, None),
            P("section", None, None),
            P("section", None, "seg"),
            P("section", None, "seg"),
            P("section", None),
            P("section", None),
            P("section", "seg", None),
            P("section", None),
            P("section", None),
        ),
        out_specs=(P("seg", "section", None, None), P("section", "seg", None), P("section", None)),
        check_vma=False,
    )
```

```python
import jax
import jax.numpy as jnp
from jax import lax
from jax.experimental import pallas as pl
from jax.experimental.pallas import tpu as pltpu
from jax.sharding import PartitionSpec as P

MEM = 16


highest = lax.Precision.HIGHEST
epsilon = 1e-05


def shifted(shard, axis, by):
    size = lax.axis_size(axis)
    return lax.ppermute(shard, axis, [(i, (i + by) % size) for i in range(size)])


def feature_map(projected):
    return jax.nn.elu(projected) + 1.0


def contract_last(left_rows, right_rows):
    return lax.dot_general(
        left_rows, right_rows, (((1,), (1,)), ((), ())), preferred_element_type=jnp.float32
    )


def contract_first(left_rows, right_rows):
    return lax.dot_general(
        left_rows,
        right_rows,
        (((0,), (0,)), ((), ())),
        precision=highest,
        preferred_element_type=jnp.float32,
    )


def visibility(starts_row):
    seg_total = starts_row.shape[0]
    positions = jnp.arange(seg_total, dtype=jnp.int32)
    last_start = lax.cummax(jnp.where(starts_row == 1, positions, jnp.int32(-1)), axis=0)
    fresh_flag = (last_start < 0).astype(jnp.float32)
    seen_pairs = (
        (positions[:, None] >= last_start[None, :]) & (positions[:, None] < positions[None, :])
    ).astype(jnp.float32)
    seen_final = (positions >= last_start[seg_total - 1]).astype(jnp.float32)
    return (fresh_flag, seen_pairs, seen_final)


def normalized(rows, gain_row):
    wide = rows.astype(jnp.float32)
    inverse_rms = lax.rsqrt(jnp.mean(wide * wide, axis=-1, keepdims=True) + epsilon)
    return (wide * inverse_rms * gain_row.astype(jnp.float32)).astype(jnp.bfloat16)


def solved(mixing, initial):
    size = mixing.shape[0]
    power = -mixing.T
    writes = initial + jnp.dot(power, initial, precision=highest)
    span = 2
    while span < size // MEM:
        power = jnp.dot(power, power, precision=highest)
        writes = writes + jnp.dot(power, writes, precision=highest)
        span *= 2
    return writes


def rows_by_rows(left, right, precision=None):
    return lax.dot_general(
        left,
        right,
        (((1,), (1,)), ((), ())),
        precision=precision,
        preferred_element_type=jnp.float32,
    )


def phi(v):
    return jnp.where(v > 0, v + 1.0, jnp.exp(jnp.minimum(v, 0.0)))


def chain_kernel(
    leaving, w_query, w_key, w_value, w_gate, gain, matrix, totals_in, starts,
    updated, matrix_out, totals_out,
    mem_rows, rows, normed, wq, wk, wv, slots, memory, keys, writes, queries, base, stage, guests,
    final, matrix_new, sims,
    load_sem, shift_send, shift_recv, slot_send, slot_recv, mem_send, mem_recv, key_send, key_recv,
    write_send, write_recv, query_send, query_recv, base_send, base_recv, store_sem,
):
    seg = lax.axis_index("seg")
    section = lax.axis_index("section")
    sections = lax.axis_size("section")
    z = seg // 2
    core = seg % 2
    pair = z + 1 - 2 * (z % 2)
    inner = (z + 1) // 2 == 1
    outer = (z + 1) // 2 != 1
    middle = jnp.where(inner, 3 - z, 3 - pair)
    far = jnp.where(inner, 3 - pair, 3 - z)
    partner = 2 * z + 1 - core
    pair_seg = 2 * pair + core
    pair_cross = 2 * pair + 1 - core
    across_seg = 2 * (3 - z) + core
    after = (section + 1) % sections
    before = (section + sections - 1) % sections
    row_count = rows.shape[0]
    width = slots.shape[1]
    part = keys.shape[2]
    seg_count = keys.shape[0]
    mem_total = memory.shape[0]
    half = width // 2

    def remote(src, dst, send, recv, to_seg, to_section=section):
        return pltpu.make_async_remote_copy(
            src_ref=src, dst_ref=dst, send_sem=send, recv_sem=recv,
            device_id=(to_seg, to_section), device_id_type=pl.DeviceIdType.MESH,
        )

    loads = [
        pltpu.make_async_copy(w_key.at[0], wk, load_sem.at[0]),
        pltpu.make_async_copy(w_value.at[0], wv, load_sem.at[1]),
        pltpu.make_async_copy(matrix.at[0], slots.at[0], load_sem.at[2]),
        pltpu.make_async_copy(w_query.at[0], wq, load_sem.at[3]),
    ]
    for load in loads:
        load.start()

    barrier = pltpu.get_barrier_semaphore()
    for to_seg, to_section in (
        (seg, after), (seg, before), (partner, section), (pair_seg, section), (pair_cross, section)
    ):
        pl.semaphore_signal(
            barrier, inc=1, device_id=(to_seg, to_section), device_id_type=pl.DeviceIdType.MESH
        )

    @pl.when(inner)
    def _():
        pl.semaphore_signal(
            barrier, inc=1, device_id=(across_seg, section), device_id_type=pl.DeviceIdType.MESH
        )
        pl.semaphore_wait(barrier, 6)

    @pl.when(outer)
    def _():
        pl.semaphore_wait(barrier, 5)

    mem_shift = remote(
        leaving.at[0, 0, pl.ds(0, MEM)], mem_rows, shift_send.at[0], shift_recv.at[0], seg, after
    )
    mem_shift.start()
    row_shift = remote(leaving.at[0, 0], rows, shift_send.at[1], shift_recv.at[1], seg, after)
    row_shift.start()

    def slot_copy(kind, piece):
        span = pl.ds(piece * half, half)
        source = slots.at[1, span] if kind == 3 else matrix.at[0, span]
        to_seg = pair_seg if kind == 1 else across_seg
        return remote(
            source, slots.at[kind, span], slot_send.at[kind - 1, piece],
            slot_recv.at[kind - 1, piece], to_seg,
        )

    @pl.when(outer)
    def _():
        slot_copy(1, 0).start()
        slot_copy(1, 1).start()

    @pl.when(inner)
    def _():
        slot_copy(2, 0).start()
        slot_copy(2, 1).start()

    same_core = [2 * chip + core for chip in (pair, middle, far)]
    other_core = [2 * chip + 1 - core for chip in (z, pair, middle, far)]

    def gather(view, send, recv):
        def copy(index, number, to_seg):
            return remote(view(index), view(index), send.at[number], recv.at[index], to_seg)

        def begin():
            copy(seg, 0, pair_seg).start()

            @pl.when(inner)
            def _():
                copy(seg, 1, across_seg).start()

            copy(seg, 2, partner).start()

        def relay():
            for k, index in enumerate(same_core):
                copy(index, 3 + k, partner).wait_recv()

                @pl.when(inner)
                def _():
                    copy(index, 6 + k, across_seg if k == 0 else pair_seg).start()

                copy(index, 3 + k, partner).start()

        def arrive():
            for index in other_core:
                copy(index, 0, partner).wait_recv()

        def finish():
            copy(seg, 0, pair_seg).wait_send()
            copy(seg, 2, partner).wait_send()
            for k, index in enumerate(same_core):
                copy(index, 3 + k, partner).wait_send()

            @pl.when(inner)
            def _():
                copy(seg, 1, across_seg).wait_send()
                for k, index in enumerate(same_core):
                    copy(index, 6 + k, pair_seg).wait_send()

        return begin, relay, arrive, finish

    gain_row = gain[...].astype(jnp.float32)

    def normalize(some):
        wide = some.astype(jnp.float32)
        scale = lax.rsqrt(jnp.mean(wide * wide, axis=-1, keepdims=True) + epsilon)
        return (wide * scale * gain_row).astype(jnp.bfloat16)

    mem_begin, mem_relay, mem_arrive, mem_finish = gather(
        lambda index: memory.at[pl.ds(pl.multiple_of(index * MEM, MEM), MEM)], mem_send, mem_recv
    )
    mem_shift.wait_recv()
    memory[pl.ds(pl.multiple_of(seg * MEM, MEM), MEM), :] = normalize(mem_rows[...])
    mem_begin()
    mem_relay()
    mem_arrive()

    key_begin, key_relay, key_arrive, key_finish = gather(
        lambda index: keys.at[index], key_send, key_recv
    )
    loads[0].wait()
    keys[seg] = phi(
        jnp.dot(memory[...], wk[...], preferred_element_type=jnp.float32)
    ).astype(jnp.bfloat16)
    key_begin()

    @pl.when(inner)
    def _():
        slot_copy(1, 0).wait_recv()
        slot_copy(3, 0).start()

    loads[1].wait()
    values = jnp.dot(memory[...], wv[...], preferred_element_type=jnp.float32)
    gate_logits = jnp.sum(
        memory[...].astype(jnp.float32) * w_gate[...].astype(jnp.float32), axis=-1, keepdims=True
    )
    rates = 1.0 / (1.0 + jnp.exp(-gate_logits))
    key_relay()
    key_arrive()

    @pl.when(inner)
    def _():
        slot_copy(1, 1).wait_recv()
        slot_copy(3, 1).start()

    def last_start(positions):
        last = jnp.full(positions.shape, -1, jnp.int32)
        for j in range(seg_count):
            last = jnp.maximum(last, jnp.where((starts[0, j] == 1) & (positions >= j), j, -1))
        return last

    square = (mem_total, mem_total)
    to_segment = lax.broadcasted_iota(jnp.int32, square, 0) // MEM
    from_segment = lax.broadcasted_iota(jnp.int32, square, 1) // MEM
    seen = ((from_segment >= last_start(to_segment)) & (from_segment < to_segment)).astype(
        jnp.float32
    )
    row_segment = lax.broadcasted_iota(jnp.int32, (mem_total, 1), 0) // MEM
    fresh_rows = (last_start(row_segment) < 0).astype(jnp.float32)
    final_segment = jnp.full((mem_total, 1), seg_count - 1, jnp.int32)
    end_last = last_start(final_segment)
    end_rows = (row_segment >= end_last).astype(jnp.float32)
    fresh_end = (end_last[:1] < 0).astype(jnp.float32)

    loads[2].wait()
    gram = jnp.zeros(square, jnp.float32)
    probed = jnp.zeros((mem_total, width), jnp.float32)
    start_scale = jnp.zeros((mem_total, 1), jnp.float32)
    for b in range(seg_count):
        cols = pl.ds(b * part, part)
        block = keys[b]
        gram += rows_by_rows(block, block)
        probed += rows_by_rows(block, slots[0, :, cols])
        start_scale += jnp.sum(
            block.astype(jnp.float32) * totals_in[:, cols], axis=-1, keepdims=True
        )
    visible = seen * gram
    scales = jnp.maximum(
        fresh_rows * start_scale + jnp.sum(visible, axis=-1, keepdims=True), 1.0
    )
    power = -(rates / scales) * visible
    solved_rows = rates * (values - (fresh_rows / scales) * probed)
    span = 1
    while span < seg_count:
        solved_rows += jnp.dot(
            power, solved_rows, precision=highest, preferred_element_type=jnp.float32
        )
        span *= 2
        if span < seg_count:
            power = jnp.dot(power, power, precision=highest, preferred_element_type=jnp.float32)
    write_begin, write_relay, write_arrive, write_finish = gather(
        lambda index: writes.at[index], write_send, write_recv
    )
    writes[seg] = solved_rows.astype(jnp.bfloat16)
    write_begin()

    row_shift.wait_recv()

    @pl.loop(0, row_count // 16)
    def _(step):
        some = pl.ds(pl.multiple_of(step * 16, 16), 16)
        normed[some, :] = normalize(rows[some, :])

    loads[3].wait()

    @pl.loop(0, seg_count)
    def _(b):
        cols = pl.ds(pl.multiple_of(b * part, part), part)
        queries[0, :, cols] = phi(
            jnp.dot(normed[...], wq[:, cols], preferred_element_type=jnp.float32)
        ).astype(jnp.bfloat16)

    query_out = remote(
        queries.at[0], queries.at[2], query_send.at[0], query_recv.at[1], pair_seg
    )

    @pl.when(outer)
    def _():
        query_out.start()

    query_swap = remote(
        queries.at[0], queries.at[1], query_send.at[1], query_recv.at[0], partner
    )
    query_swap.start()
    write_relay()

    ended = (solved_rows * end_rows).T
    for b in range(seg_count):
        cols = pl.ds(b * part, part)
        block = keys[b].astype(jnp.float32)
        matrix_new[:, cols] = (
            fresh_end * slots[0, :, cols].astype(jnp.float32)
            + jnp.dot(ended, block, precision=highest, preferred_element_type=jnp.float32)
        ).astype(jnp.bfloat16)
        totals_out[:, cols] = fresh_end * totals_in[:, cols] + jnp.sum(
            end_rows * block, axis=0, keepdims=True
        )
    matrix_store = pltpu.make_async_copy(matrix_new, matrix_out.at[0], store_sem.at[0])
    matrix_store.start()

    key_segment = lax.broadcasted_iota(jnp.int32, (1, mem_total), 1) // MEM
    my_segment = jnp.full((1, mem_total), 0, jnp.int32) + seg
    my_last = last_start(my_segment)
    my_mask = ((key_segment >= my_last) & (key_segment < my_segment)).astype(jnp.float32)
    my_fresh = (my_last[:, :1] < 0).astype(jnp.float32)
    similarity = jnp.zeros((row_count, mem_total), jnp.float32)
    query_scale = jnp.zeros((row_count, 1), jnp.float32)
    for b in range(seg_count):
        cols = pl.ds(b * part, part)
        mine = queries[0, :, cols]
        similarity += rows_by_rows(mine, keys[b])
        query_scale += jnp.sum(
            mine.astype(jnp.float32) * totals_in[:, cols], axis=-1, keepdims=True
        )
    similarity *= my_mask
    inverse = 1.0 / jnp.maximum(
        my_fresh * query_scale + jnp.sum(similarity, axis=-1, keepdims=True), 1.0
    )
    sims[...] = similarity.astype(jnp.bfloat16)
    my_scale = my_fresh * inverse

    def read(rows_at, slot):
        return rows_by_rows(queries[rows_at], slots[slot]).astype(jnp.bfloat16)

    def partner_copy(slot, column):
        return remote(
            stage.at[slot], base.at[column], base_send.at[slot], base_recv.at[column], partner
        )

    guest_slots = (0, 2, 3)

    def guest_copy(number, which, column):
        return remote(
            guests.at[2 * number + which], base.at[column], base_send.at[4 + 2 * number + which],
            base_recv.at[column], pair_cross if which else pair_seg,
        )

    def chip_read(slot, column):
        stage[slot] = read(1, slot)
        partner_copy(slot, column).start()
        base[column] = read(0, slot)

    def guest_read(number, column):
        for which in range(2):
            guests[2 * number + which] = read(2 + which, guest_slots[number])
            guest_copy(number, which, column).start()

    query_swap.wait_recv()
    chip_read(0, seg)
    guest_swap = remote(
        queries.at[2], queries.at[3], query_send.at[2], query_recv.at[2], partner
    )

    @pl.when(inner)
    def _():
        chip_read(1, same_core[0])
        slot_copy(2, 0).wait_recv()
        slot_copy(2, 1).wait_recv()
        chip_read(2, same_core[1])
        query_out.wait_recv()
        guest_swap.start()
        guest_swap.wait_recv()
        guest_read(0, seg)
        guest_read(1, same_core[1])
        slot_copy(3, 0).wait_recv()
        slot_copy(3, 1).wait_recv()
        guest_read(2, same_core[2])
        chip_read(3, same_core[2])

    write_arrive()

    def combine(column):
        cols = pl.ds(pl.multiple_of(column * width, width), width)
        low = jnp.dot(sims[...], writes[column], preferred_element_type=jnp.float32)
        final[:, cols] = (
            rows[:, cols].astype(jnp.float32)
            + my_scale * base[column].astype(jnp.float32)
            + inverse * low
        ).astype(jnp.bfloat16)
        return pltpu.make_async_copy(
            final.at[:, cols], updated.at[0, 0, :, cols], store_sem.at[1 + column]
        )

    stores = [combine(seg)]
    stores[0].start()

    def landed(column):
        partner_copy(0, column).wait_recv()

    landed(partner)
    stores.append(combine(partner))
    stores[-1].start()
    for k in range(3):
        @pl.when(outer)
        def _():
            landed(same_core[k])

        stores.append(combine(same_core[k]))
        stores[-1].start()
        landed(other_core[k + 1])
        stores.append(combine(other_core[k + 1]))
        stores[-1].start()

    mem_shift.wait_send()
    row_shift.wait_send()
    query_swap.wait_send()
    partner_copy(0, seg).wait_send()

    @pl.when(outer)
    def _():
        slot_copy(1, 0).wait_send()
        slot_copy(1, 1).wait_send()
        query_out.wait_send()

    @pl.when(inner)
    def _():
        for piece in range(2):
            slot_copy(2, piece).wait_send()
            slot_copy(3, piece).wait_send()
        guest_swap.wait_send()
        for slot in (1, 2, 3):
            partner_copy(slot, seg).wait_send()
        for number in range(3):
            for which in range(2):
                guest_copy(number, which, seg).wait_send()

    mem_finish()
    key_finish()
    write_finish()
    matrix_store.wait()
    for store in stores:
        store.wait()


def chained(
    leaving, w_query, w_key, w_value, w_gate, norm_gain, memory_matrix, key_totals, doc_starts
):
    seg_count = lax.axis_size("seg")
    rows, features = leaving.shape[2:]
    key_width = w_query.shape[2]
    part = w_key.shape[2]
    width = memory_matrix.shape[1]
    mem_total = seg_count * MEM
    short = jnp.bfloat16
    anywhere = pl.BlockSpec(memory_space=pl.ANY)
    near = pl.BlockSpec(memory_space=pltpu.VMEM)
    dma = pltpu.SemaphoreType.DMA
    updated, matrix_next, totals_next = pl.pallas_call(
        chain_kernel,
        out_shape=(
            jax.ShapeDtypeStruct(leaving.shape, short),
            jax.ShapeDtypeStruct(memory_matrix.shape, short),
            jax.ShapeDtypeStruct(key_totals.shape, jnp.float32),
        ),
        in_specs=[
            anywhere, anywhere, anywhere, anywhere, near, near, anywhere, near,
            pl.BlockSpec(memory_space=pltpu.SMEM),
        ],
        out_specs=(anywhere, anywhere, near),
        scratch_shapes=[
            pltpu.VMEM((MEM, features), short),
            pltpu.VMEM((rows, features), short),
            pltpu.VMEM((rows, features), short),
            pltpu.VMEM((features, key_width), short),
            pltpu.VMEM((features, part), short),
            pltpu.VMEM((features, width), short),
            pltpu.VMEM((4, width, key_width), short),
            pltpu.VMEM((mem_total, features), short),
            pltpu.VMEM((seg_count, mem_total, part), short),
            pltpu.VMEM((seg_count, mem_total, width), short),
            pltpu.VMEM((4, rows, key_width), short),
            pltpu.VMEM((seg_count, rows, width), short),
            pltpu.VMEM((4, rows, width), short),
            pltpu.VMEM((6, rows, width), short),
            pltpu.VMEM((rows, features), short),
            pltpu.VMEM((width, key_width), short),
            pltpu.VMEM((rows, mem_total), short),
            dma((4,)), dma((2,)), dma((2,)), dma((3, 2)), dma((3, 2)),
            dma((9,)), dma((seg_count,)), dma((9,)), dma((seg_count,)),
            dma((9,)), dma((seg_count,)), dma((3,)), dma((3,)),
            dma((10,)), dma((seg_count,)), dma((1 + seg_count,)),
        ],
        compiler_params=pltpu.CompilerParams(
            collective_id=0, has_side_effects=True, vmem_limit_bytes=63 * 1024 * 1024
        ),
    )(
        leaving, w_query, w_key, w_value, w_gate, norm_gain, memory_matrix, key_totals, doc_starts
    )
    return (updated, matrix_next, totals_next)


def local(
    leaving, w_query, w_key, w_value, w_gate, norm_gain, memory_matrix, key_totals, doc_starts
):
    seg_count = lax.axis_size("seg")
    my_index = lax.axis_index("seg")
    memory_rows = shifted(leaving[0, 0, :MEM], "section", 1)
    entering = shifted(leaving, "section", 1)[0, 0]
    matrix = memory_matrix[0]
    whole_matrix = lax.all_gather(matrix, "seg", axis=0, tiled=True)
    memory = lax.all_gather(normalized(memory_rows, norm_gain[0]), "seg", axis=0, tiled=True)
    key_part = feature_map(jnp.dot(memory, w_key[0], preferred_element_type=jnp.float32)).astype(
        jnp.bfloat16
    )
    value_part = jnp.dot(memory, w_value[0], preferred_element_type=jnp.float32)
    gate_rates = jax.nn.sigmoid(jnp.dot(memory, w_gate[0], preferred_element_type=jnp.float32))
    key_rows = lax.all_gather(key_part, "seg", axis=1, tiled=True)
    fresh_flag, seen_pairs, seen_final = visibility(doc_starts[0])
    key_wide = key_rows.astype(jnp.float32)
    key_sums = key_wide.reshape(seg_count, MEM, -1).sum(axis=1)
    totals = fresh_flag[:, None] * key_totals[0][None, :] + jnp.dot(
        seen_pairs.T, key_sums, precision=highest
    )
    total_rows = jnp.repeat(totals, MEM, axis=0)
    key_scales = jnp.maximum(jnp.sum(total_rows * key_wide, axis=-1), 1.0)
    key_gram = contract_last(key_rows, key_rows)
    seen_cols = jnp.repeat(jnp.repeat(seen_pairs, MEM, axis=0), MEM, axis=1)
    mixing = seen_cols * key_gram * (gate_rates / key_scales)[None, :]
    fresh_rows = jnp.repeat(fresh_flag, MEM)
    probed_keys = contract_last(key_rows, matrix)
    initial = gate_rates[:, None] * (
        value_part - (fresh_rows / key_scales)[:, None] * probed_keys
    )
    write_cols = solved(mixing, initial)
    writes = lax.all_gather(write_cols.astype(jnp.bfloat16), "seg", axis=1, tiled=True)
    fresh_end = fresh_flag[seg_count - 1]
    end_rows = jnp.repeat(seen_final, MEM)
    matrix_next = (
        fresh_end * matrix.astype(jnp.float32)
        + contract_first(write_cols * end_rows[:, None], key_wide)
    ).astype(jnp.bfloat16)
    totals_next = fresh_end * key_totals[0] + jnp.dot(seen_final, key_sums, precision=highest)
    normed = normalized(entering, norm_gain[0])
    queries = feature_map(jnp.dot(normed, w_query[0], preferred_element_type=jnp.float32)).astype(
        jnp.bfloat16
    )
    my_fresh = fresh_flag[my_index]
    column_mask = jnp.repeat(seen_pairs[:, my_index], MEM)
    my_totals = lax.dynamic_slice_in_dim(totals, my_index, 1, 0)
    denominator = jnp.maximum(jnp.sum(queries.astype(jnp.float32) * my_totals, axis=-1), 1.0)
    similarity = contract_last(queries, key_rows) * column_mask[None, :]
    low_rank = jnp.dot(
        similarity.astype(jnp.bfloat16), writes, preferred_element_type=jnp.float32
    )
    base_read = contract_last(queries, whole_matrix)
    updated = (
        entering.astype(jnp.float32) + (my_fresh * base_read + low_rank) / denominator[:, None]
    ).astype(jnp.bfloat16)
    return (updated[None, None], matrix_next[None], totals_next[None])


def solution(mesh):
    fits = mesh.shape["seg"] == 8 and mesh.shape["section"] > 2
    return jax.shard_map(
        chained if fits else local,
        mesh=mesh,
        in_specs=(
            P("seg", "section", None, None),
            P("section", None, None),
            P("section", None, "seg"),
            P("section", None, "seg"),
            P("section", None),
            P("section", None),
            P("section", "seg", None),
            P("section", None),
            P("section", None),
        ),
        out_specs=(P("seg", "section", None, None), P("section", "seg", None), P("section", None)),
        check_vma=False,
    )
```

```python
import jax
import jax.numpy as jnp
from jax import lax
from jax.experimental import pallas as pl
from jax.experimental.pallas import tpu as pltpu
from jax.sharding import PartitionSpec as P

MEM = 16


highest = lax.Precision.HIGHEST
epsilon = 1e-05


def shifted(shard, axis, by):
    size = lax.axis_size(axis)
    return lax.ppermute(shard, axis, [(i, (i + by) % size) for i in range(size)])


def feature_map(projected):
    return jax.nn.elu(projected) + 1.0


def contract_last(left_rows, right_rows):
    return lax.dot_general(
        left_rows, right_rows, (((1,), (1,)), ((), ())), preferred_element_type=jnp.float32
    )


def contract_first(left_rows, right_rows):
    return lax.dot_general(
        left_rows,
        right_rows,
        (((0,), (0,)), ((), ())),
        precision=highest,
        preferred_element_type=jnp.float32,
    )


def visibility(starts_row):
    seg_total = starts_row.shape[0]
    positions = jnp.arange(seg_total, dtype=jnp.int32)
    last_start = lax.cummax(jnp.where(starts_row == 1, positions, jnp.int32(-1)), axis=0)
    fresh_flag = (last_start < 0).astype(jnp.float32)
    seen_pairs = (
        (positions[:, None] >= last_start[None, :]) & (positions[:, None] < positions[None, :])
    ).astype(jnp.float32)
    seen_final = (positions >= last_start[seg_total - 1]).astype(jnp.float32)
    return (fresh_flag, seen_pairs, seen_final)


def normalized(rows, gain_row):
    wide = rows.astype(jnp.float32)
    inverse_rms = lax.rsqrt(jnp.mean(wide * wide, axis=-1, keepdims=True) + epsilon)
    return (wide * inverse_rms * gain_row.astype(jnp.float32)).astype(jnp.bfloat16)


def solved(mixing, initial):
    size = mixing.shape[0]
    power = -mixing.T
    writes = initial + jnp.dot(power, initial, precision=highest)
    span = 2
    while span < size // MEM:
        power = jnp.dot(power, power, precision=highest)
        writes = writes + jnp.dot(power, writes, precision=highest)
        span *= 2
    return writes


def rows_by_rows(left, right, precision=None):
    return lax.dot_general(
        left,
        right,
        (((1,), (1,)), ((), ())),
        precision=precision,
        preferred_element_type=jnp.float32,
    )


def phi(v):
    return jnp.where(v > 0, v + 1.0, jnp.exp(jnp.minimum(v, 0.0)))


def chain_kernel(
    leaving, w_query, w_key, w_value, w_gate, gain, matrix, totals_in, starts,
    updated, matrix_out, totals_out,
    mem_rows, rows, normed, wq, wk, wv, slots, memory, keys, writes, queries, base, stage, guests,
    final, matrix_new, sims,
    load_sem, shift_send, shift_recv, slot_send, slot_recv, mem_send, mem_recv, key_send, key_recv,
    write_send, write_recv, query_send, query_recv, base_send, base_recv, store_sem,
):
    seg = lax.axis_index("seg")
    section = lax.axis_index("section")
    sections = lax.axis_size("section")
    z = seg // 2
    core = seg % 2
    pair = z + 1 - 2 * (z % 2)
    inner = (z + 1) // 2 == 1
    outer = (z + 1) // 2 != 1
    middle = jnp.where(inner, 3 - z, 3 - pair)
    far = jnp.where(inner, 3 - pair, 3 - z)
    partner = 2 * z + 1 - core
    pair_seg = 2 * pair + core
    pair_cross = 2 * pair + 1 - core
    across_seg = 2 * (3 - z) + core
    after = (section + 1) % sections
    before = (section + sections - 1) % sections
    row_count = rows.shape[0]
    width = slots.shape[1]
    part = keys.shape[2]
    seg_count = keys.shape[0]
    mem_total = memory.shape[0]
    half = width // 2
    pieces = slot_send.shape[1]
    depth = width // pieces

    def remote(src, dst, send, recv, to_seg, to_section=section):
        return pltpu.make_async_remote_copy(
            src_ref=src, dst_ref=dst, send_sem=send, recv_sem=recv,
            device_id=(to_seg, to_section), device_id_type=pl.DeviceIdType.MESH,
        )

    loads = [
        pltpu.make_async_copy(w_key.at[0], wk, load_sem.at[0]),
        pltpu.make_async_copy(w_value.at[0], wv, load_sem.at[1]),
        pltpu.make_async_copy(matrix.at[0], slots.at[0], load_sem.at[2]),
        pltpu.make_async_copy(w_query.at[0], wq, load_sem.at[3]),
    ]
    for load in loads:
        load.start()

    barrier = pltpu.get_barrier_semaphore()
    for to_seg, to_section in (
        (seg, after), (seg, before), (partner, section), (pair_seg, section), (pair_cross, section)
    ):
        pl.semaphore_signal(
            barrier, inc=1, device_id=(to_seg, to_section), device_id_type=pl.DeviceIdType.MESH
        )

    @pl.when(inner)
    def _():
        pl.semaphore_signal(
            barrier, inc=1, device_id=(across_seg, section), device_id_type=pl.DeviceIdType.MESH
        )
        pl.semaphore_wait(barrier, 6)

    @pl.when(outer)
    def _():
        pl.semaphore_wait(barrier, 5)

    mem_shift = remote(
        leaving.at[0, 0, pl.ds(0, MEM)], mem_rows, shift_send.at[0], shift_recv.at[0], seg, after
    )
    mem_shift.start()
    row_shift = remote(leaving.at[0, 0], rows, shift_send.at[1], shift_recv.at[1], seg, after)
    row_shift.start()

    def slot_copy(kind, piece):
        span = pl.ds(piece * depth, depth)
        source = slots.at[1, span] if kind == 3 else matrix.at[0, span]
        to_seg = pair_seg if kind == 1 else across_seg
        return remote(
            source, slots.at[kind, span], slot_send.at[kind - 1, piece],
            slot_recv.at[kind - 1, piece], to_seg,
        )

    def pump(first, last):
        for number in range(first, last):
            if number < pieces:
                @pl.when(outer)
                def _():
                    slot_copy(1, number).start()

                @pl.when(inner)
                def _():
                    slot_copy(2, number).start()
            else:
                @pl.when(inner)
                def _():
                    slot_copy(1, number - pieces).wait_recv()
                    slot_copy(3, number - pieces).start()

    pump(0, 1)

    same_core = [2 * chip + core for chip in (pair, middle, far)]
    other_core = [2 * chip + 1 - core for chip in (z, pair, middle, far)]

    def gather(view, send, recv):
        def copy(index, number, to_seg):
            return remote(view(index), view(index), send.at[number], recv.at[index], to_seg)

        def begin():
            copy(seg, 0, pair_seg).start()

            @pl.when(inner)
            def _():
                copy(seg, 1, across_seg).start()

            copy(seg, 2, partner).start()

        def relay(k):
            index = same_core[k]
            copy(index, 3 + k, partner).wait_recv()

            @pl.when(inner)
            def _():
                copy(index, 6 + k, across_seg if k == 0 else pair_seg).start()

            copy(index, 3 + k, partner).start()

        def arrive():
            for index in other_core:
                copy(index, 0, partner).wait_recv()

        def finish():
            copy(seg, 0, pair_seg).wait_send()
            copy(seg, 2, partner).wait_send()
            for k, index in enumerate(same_core):
                copy(index, 3 + k, partner).wait_send()

            @pl.when(inner)
            def _():
                copy(seg, 1, across_seg).wait_send()
                for k, index in enumerate(same_core):
                    copy(index, 6 + k, pair_seg).wait_send()

        return begin, relay, arrive, finish

    gain_row = gain[...].astype(jnp.float32)

    def normalize(some):
        wide = some.astype(jnp.float32)
        scale = lax.rsqrt(jnp.mean(wide * wide, axis=-1, keepdims=True) + epsilon)
        return (wide * scale * gain_row).astype(jnp.bfloat16)

    mem_begin, mem_relay, mem_arrive, mem_finish = gather(
        lambda index: memory.at[pl.ds(pl.multiple_of(index * MEM, MEM), MEM)], mem_send, mem_recv
    )
    mem_shift.wait_recv()
    memory[pl.ds(pl.multiple_of(seg * MEM, MEM), MEM), :] = normalize(mem_rows[...])
    mem_begin()
    for k in range(3):
        pump(1 + k, 2 + k)
        mem_relay(k)
    pump(4, 5)
    mem_arrive()

    key_begin, key_relay, key_arrive, key_finish = gather(
        lambda index: keys.at[index], key_send, key_recv
    )
    loads[0].wait()
    keys[seg] = phi(
        jnp.dot(memory[...], wk[...], preferred_element_type=jnp.float32)
    ).astype(jnp.bfloat16)
    key_begin()
    pump(5, 6)
    loads[1].wait()
    values = jnp.dot(memory[...], wv[...], preferred_element_type=jnp.float32)
    gate_logits = jnp.sum(
        memory[...].astype(jnp.float32) * w_gate[...].astype(jnp.float32), axis=-1, keepdims=True
    )
    rates = 1.0 / (1.0 + jnp.exp(-gate_logits))
    for k in range(3):
        key_relay(k)
        pump(6 + k, 7 + k)
    key_arrive()
    pump(9, 12)

    row_shift.wait_recv()

    @pl.loop(0, row_count // 16)
    def _(step):
        some = pl.ds(pl.multiple_of(step * 16, 16), 16)
        normed[some, :] = normalize(rows[some, :])

    loads[3].wait()

    @pl.loop(0, seg_count)
    def _(b):
        cols = pl.ds(pl.multiple_of(b * part, part), part)
        queries[0, :, cols] = phi(
            jnp.dot(normed[...], wq[:, cols], preferred_element_type=jnp.float32)
        ).astype(jnp.bfloat16)

    query_out = remote(
        queries.at[0], queries.at[2], query_send.at[0], query_recv.at[1], pair_seg
    )

    @pl.when(outer)
    def _():
        query_out.start()

    query_swap = remote(
        queries.at[0], queries.at[1], query_send.at[1], query_recv.at[0], partner
    )
    query_swap.start()
    pump(12, 14)

    def last_start(positions):
        last = jnp.full(positions.shape, -1, jnp.int32)
        for j in range(seg_count):
            last = jnp.maximum(last, jnp.where((starts[0, j] == 1) & (positions >= j), j, -1))
        return last

    square = (mem_total, mem_total)
    to_segment = lax.broadcasted_iota(jnp.int32, square, 0) // MEM
    from_segment = lax.broadcasted_iota(jnp.int32, square, 1) // MEM
    seen = ((from_segment >= last_start(to_segment)) & (from_segment < to_segment)).astype(
        jnp.float32
    )
    row_segment = lax.broadcasted_iota(jnp.int32, (mem_total, 1), 0) // MEM
    fresh_rows = (last_start(row_segment) < 0).astype(jnp.float32)
    final_segment = jnp.full((mem_total, 1), seg_count - 1, jnp.int32)
    end_last = last_start(final_segment)
    end_rows = (row_segment >= end_last).astype(jnp.float32)
    fresh_end = (end_last[:1] < 0).astype(jnp.float32)

    loads[2].wait()
    gram = jnp.zeros(square, jnp.float32)
    probed = jnp.zeros((mem_total, width), jnp.float32)
    start_scale = jnp.zeros((mem_total, 1), jnp.float32)
    for b in range(seg_count):
        cols = pl.ds(b * part, part)
        block = keys[b]
        gram += rows_by_rows(block, block)
        probed += rows_by_rows(block, slots[0, :, cols])
        start_scale += jnp.sum(
            block.astype(jnp.float32) * totals_in[:, cols], axis=-1, keepdims=True
        )
    visible = seen * gram
    scales = jnp.maximum(
        fresh_rows * start_scale + jnp.sum(visible, axis=-1, keepdims=True), 1.0
    )
    power = -(rates / scales) * visible
    solved_rows = rates * (values - (fresh_rows / scales) * probed)
    span = 1
    while span < seg_count:
        solved_rows += jnp.dot(
            power, solved_rows, precision=highest, preferred_element_type=jnp.float32
        )
        span *= 2
        if span < seg_count:
            power = jnp.dot(power, power, precision=highest, preferred_element_type=jnp.float32)
    write_begin, write_relay, write_arrive, write_finish = gather(
        lambda index: writes.at[index], write_send, write_recv
    )
    writes[seg] = solved_rows.astype(jnp.bfloat16)
    write_begin()

    pump(14, 2 * pieces)
    key_segment = lax.broadcasted_iota(jnp.int32, (1, mem_total), 1) // MEM
    my_segment = jnp.full((1, mem_total), 0, jnp.int32) + seg
    my_last = last_start(my_segment)
    my_mask = ((key_segment >= my_last) & (key_segment < my_segment)).astype(jnp.float32)
    my_fresh = (my_last[:, :1] < 0).astype(jnp.float32)
    similarity = jnp.zeros((row_count, mem_total), jnp.float32)
    query_scale = jnp.zeros((row_count, 1), jnp.float32)
    for b in range(seg_count):
        cols = pl.ds(b * part, part)
        mine = queries[0, :, cols]
        similarity += rows_by_rows(mine, keys[b])
        query_scale += jnp.sum(
            mine.astype(jnp.float32) * totals_in[:, cols], axis=-1, keepdims=True
        )
    similarity *= my_mask
    inverse = 1.0 / jnp.maximum(
        my_fresh * query_scale + jnp.sum(similarity, axis=-1, keepdims=True), 1.0
    )
    sims[...] = similarity.astype(jnp.bfloat16)
    my_scale = my_fresh * inverse

    write_relay(0)

    ended = (solved_rows * end_rows).T
    for b in range(seg_count):
        cols = pl.ds(b * part, part)
        block = keys[b].astype(jnp.float32)
        matrix_new[:, cols] = (
            fresh_end * slots[0, :, cols].astype(jnp.float32)
            + jnp.dot(ended, block, precision=highest, preferred_element_type=jnp.float32)
        ).astype(jnp.bfloat16)
        totals_out[:, cols] = fresh_end * totals_in[:, cols] + jnp.sum(
            end_rows * block, axis=0, keepdims=True
        )
    matrix_store = pltpu.make_async_copy(matrix_new, matrix_out.at[0], store_sem.at[0])
    matrix_store.start()

    write_relay(1)

    def read(rows_at, slot):
        return rows_by_rows(queries[rows_at], slots[slot]).astype(jnp.bfloat16)

    def read_half(rows_at, h):
        return rows_by_rows(queries[rows_at], slots[3, pl.ds(h * half, half)]).astype(
            jnp.bfloat16
        )

    def partner_copy(slot, column):
        return remote(
            stage.at[slot], base.at[column], base_send.at[slot], base_recv.at[column, 0], partner
        )

    def partner_half(h, column):
        cols = pl.ds(h * half, half)
        return remote(
            stage.at[3, :, cols], base.at[column, :, cols], base_send.at[10 + h],
            base_recv.at[column, h], partner,
        )

    guest_slots = (0, 2)

    def guest_copy(number, which, column):
        return remote(
            guests.at[2 * number + which], base.at[column], base_send.at[4 + 2 * number + which],
            base_recv.at[column, 0], pair_cross if which else pair_seg,
        )

    def guest_half(h, which, column):
        cols = pl.ds(h * half, half)
        return remote(
            guests.at[4 + which, :, cols], base.at[column, :, cols],
            base_send.at[12 + 2 * h + which], base_recv.at[column, h],
            pair_cross if which else pair_seg,
        )

    def far_read(h, column):
        cols = pl.ds(h * half, half)
        for piece in range(h * pieces // 2, (h + 1) * pieces // 2):
            slot_copy(3, piece).wait_recv()
        for which in range(2):
            guests[4 + which, :, cols] = read_half(2 + which, h)
            guest_half(h, which, column).start()
        stage[3, :, cols] = read_half(1, h)
        partner_half(h, column).start()
        base[column, :, cols] = read_half(0, h)

    def chip_read(slot, column):
        stage[slot] = read(1, slot)
        partner_copy(slot, column).start()
        base[column] = read(0, slot)

    def guest_read(number, column):
        for which in range(2):
            guests[2 * number + which] = read(2 + which, guest_slots[number])
            guest_copy(number, which, column).start()

    query_swap.wait_recv()
    chip_read(0, seg)
    write_relay(2)
    guest_swap = remote(
        queries.at[2], queries.at[3], query_send.at[2], query_recv.at[2], partner
    )

    @pl.when(inner)
    def _():
        chip_read(1, same_core[0])
        for piece in range(pieces):
            slot_copy(2, piece).wait_recv()
        chip_read(2, same_core[1])
        query_out.wait_recv()
        guest_swap.start()
        guest_swap.wait_recv()
        guest_read(0, seg)
        guest_read(1, same_core[1])
        far_read(0, same_core[2])
        far_read(1, same_core[2])

    write_arrive()

    def combine(column):
        cols = pl.ds(pl.multiple_of(column * width, width), width)
        low = jnp.dot(sims[...], writes[column], preferred_element_type=jnp.float32)
        final[:, cols] = (
            rows[:, cols].astype(jnp.float32)
            + my_scale * base[column].astype(jnp.float32)
            + inverse * low
        ).astype(jnp.bfloat16)
        return pltpu.make_async_copy(
            final.at[:, cols], updated.at[0, 0, :, cols], store_sem.at[1 + column]
        )

    stores = [combine(seg)]
    stores[0].start()

    def landed(column, halves=False):
        if halves:
            partner_half(0, column).wait_recv()
            partner_half(1, column).wait_recv()
        else:
            partner_copy(0, column).wait_recv()

    landed(partner)
    stores.append(combine(partner))
    stores[-1].start()
    for k in range(3):
        @pl.when(outer)
        def _():
            landed(same_core[k], k == 2)

        stores.append(combine(same_core[k]))
        stores[-1].start()
        landed(other_core[k + 1], k == 2)
        stores.append(combine(other_core[k + 1]))
        stores[-1].start()

    mem_shift.wait_send()
    row_shift.wait_send()
    query_swap.wait_send()
    partner_copy(0, seg).wait_send()

    @pl.when(outer)
    def _():
        for piece in range(pieces):
            slot_copy(1, piece).wait_send()
        query_out.wait_send()

    @pl.when(inner)
    def _():
        for piece in range(pieces):
            slot_copy(2, piece).wait_send()
            slot_copy(3, piece).wait_send()
        guest_swap.wait_send()
        for slot in (1, 2):
            partner_copy(slot, seg).wait_send()
        for which in range(2):
            for number in range(2):
                guest_copy(number, which, seg).wait_send()
            partner_half(which, seg).wait_send()
            for h in range(2):
                guest_half(h, which, seg).wait_send()

    mem_finish()
    key_finish()
    write_finish()
    matrix_store.wait()
    for store in stores:
        store.wait()


def chained(
    leaving, w_query, w_key, w_value, w_gate, norm_gain, memory_matrix, key_totals, doc_starts
):
    seg_count = lax.axis_size("seg")
    rows, features = leaving.shape[2:]
    key_width = w_query.shape[2]
    part = w_key.shape[2]
    width = memory_matrix.shape[1]
    mem_total = seg_count * MEM
    short = jnp.bfloat16
    anywhere = pl.BlockSpec(memory_space=pl.ANY)
    near = pl.BlockSpec(memory_space=pltpu.VMEM)
    dma = pltpu.SemaphoreType.DMA
    updated, matrix_next, totals_next = pl.pallas_call(
        chain_kernel,
        out_shape=(
            jax.ShapeDtypeStruct(leaving.shape, short),
            jax.ShapeDtypeStruct(memory_matrix.shape, short),
            jax.ShapeDtypeStruct(key_totals.shape, jnp.float32),
        ),
        in_specs=[
            anywhere, anywhere, anywhere, anywhere, near, near, anywhere, near,
            pl.BlockSpec(memory_space=pltpu.SMEM),
        ],
        out_specs=(anywhere, anywhere, near),
        scratch_shapes=[
            pltpu.VMEM((MEM, features), short),
            pltpu.VMEM((rows, features), short),
            pltpu.VMEM((rows, features), short),
            pltpu.VMEM((features, key_width), short),
            pltpu.VMEM((features, part), short),
            pltpu.VMEM((features, width), short),
            pltpu.VMEM((4, width, key_width), short),
            pltpu.VMEM((mem_total, features), short),
            pltpu.VMEM((seg_count, mem_total, part), short),
            pltpu.VMEM((seg_count, mem_total, width), short),
            pltpu.VMEM((4, rows, key_width), short),
            pltpu.VMEM((seg_count, rows, width), short),
            pltpu.VMEM((4, rows, width), short),
            pltpu.VMEM((6, rows, width), short),
            pltpu.VMEM((rows, features), short),
            pltpu.VMEM((width, key_width), short),
            pltpu.VMEM((rows, mem_total), short),
            dma((4,)), dma((2,)), dma((2,)), dma((3, 8)), dma((3, 8)),
            dma((9,)), dma((seg_count,)), dma((9,)), dma((seg_count,)),
            dma((9,)), dma((seg_count,)), dma((3,)), dma((3,)),
            dma((16,)), dma((seg_count, 2)), dma((1 + seg_count,)),
        ],
        compiler_params=pltpu.CompilerParams(
            collective_id=0, has_side_effects=True, vmem_limit_bytes=63 * 1024 * 1024
        ),
    )(
        leaving, w_query, w_key, w_value, w_gate, norm_gain, memory_matrix, key_totals, doc_starts
    )
    return (updated, matrix_next, totals_next)


def local(
    leaving, w_query, w_key, w_value, w_gate, norm_gain, memory_matrix, key_totals, doc_starts
):
    seg_count = lax.axis_size("seg")
    my_index = lax.axis_index("seg")
    memory_rows = shifted(leaving[0, 0, :MEM], "section", 1)
    entering = shifted(leaving, "section", 1)[0, 0]
    matrix = memory_matrix[0]
    whole_matrix = lax.all_gather(matrix, "seg", axis=0, tiled=True)
    memory = lax.all_gather(normalized(memory_rows, norm_gain[0]), "seg", axis=0, tiled=True)
    key_part = feature_map(jnp.dot(memory, w_key[0], preferred_element_type=jnp.float32)).astype(
        jnp.bfloat16
    )
    value_part = jnp.dot(memory, w_value[0], preferred_element_type=jnp.float32)
    gate_rates = jax.nn.sigmoid(jnp.dot(memory, w_gate[0], preferred_element_type=jnp.float32))
    key_rows = lax.all_gather(key_part, "seg", axis=1, tiled=True)
    fresh_flag, seen_pairs, seen_final = visibility(doc_starts[0])
    key_wide = key_rows.astype(jnp.float32)
    key_sums = key_wide.reshape(seg_count, MEM, -1).sum(axis=1)
    totals = fresh_flag[:, None] * key_totals[0][None, :] + jnp.dot(
        seen_pairs.T, key_sums, precision=highest
    )
    total_rows = jnp.repeat(totals, MEM, axis=0)
    key_scales = jnp.maximum(jnp.sum(total_rows * key_wide, axis=-1), 1.0)
    key_gram = contract_last(key_rows, key_rows)
    seen_cols = jnp.repeat(jnp.repeat(seen_pairs, MEM, axis=0), MEM, axis=1)
    mixing = seen_cols * key_gram * (gate_rates / key_scales)[None, :]
    fresh_rows = jnp.repeat(fresh_flag, MEM)
    probed_keys = contract_last(key_rows, matrix)
    initial = gate_rates[:, None] * (
        value_part - (fresh_rows / key_scales)[:, None] * probed_keys
    )
    write_cols = solved(mixing, initial)
    writes = lax.all_gather(write_cols.astype(jnp.bfloat16), "seg", axis=1, tiled=True)
    fresh_end = fresh_flag[seg_count - 1]
    end_rows = jnp.repeat(seen_final, MEM)
    matrix_next = (
        fresh_end * matrix.astype(jnp.float32)
        + contract_first(write_cols * end_rows[:, None], key_wide)
    ).astype(jnp.bfloat16)
    totals_next = fresh_end * key_totals[0] + jnp.dot(seen_final, key_sums, precision=highest)
    normed = normalized(entering, norm_gain[0])
    queries = feature_map(jnp.dot(normed, w_query[0], preferred_element_type=jnp.float32)).astype(
        jnp.bfloat16
    )
    my_fresh = fresh_flag[my_index]
    column_mask = jnp.repeat(seen_pairs[:, my_index], MEM)
    my_totals = lax.dynamic_slice_in_dim(totals, my_index, 1, 0)
    denominator = jnp.maximum(jnp.sum(queries.astype(jnp.float32) * my_totals, axis=-1), 1.0)
    similarity = contract_last(queries, key_rows) * column_mask[None, :]
    low_rank = jnp.dot(
        similarity.astype(jnp.bfloat16), writes, preferred_element_type=jnp.float32
    )
    base_read = contract_last(queries, whole_matrix)
    updated = (
        entering.astype(jnp.float32) + (my_fresh * base_read + low_rank) / denominator[:, None]
    ).astype(jnp.bfloat16)
    return (updated[None, None], matrix_next[None], totals_next[None])


def solution(mesh):
    fits = mesh.shape["seg"] == 8 and mesh.shape["section"] > 2
    return jax.shard_map(
        chained if fits else local,
        mesh=mesh,
        in_specs=(
            P("seg", "section", None, None),
            P("section", None, None),
            P("section", None, "seg"),
            P("section", None, "seg"),
            P("section", None),
            P("section", None),
            P("section", "seg", None),
            P("section", None),
            P("section", None),
        ),
        out_specs=(P("seg", "section", None, None), P("section", "seg", None), P("section", None)),
        check_vma=False,
    )
```

```python
import jax
import jax.numpy as jnp
from jax import lax
from jax.experimental import pallas as pl
from jax.experimental.pallas import tpu as pltpu
from jax.sharding import PartitionSpec as P

MEM = 16


highest = lax.Precision.HIGHEST
epsilon = 1e-05


def shifted(shard, axis, by):
    size = lax.axis_size(axis)
    return lax.ppermute(shard, axis, [(i, (i + by) % size) for i in range(size)])


def feature_map(projected):
    return jax.nn.elu(projected) + 1.0


def contract_last(left_rows, right_rows):
    return lax.dot_general(
        left_rows, right_rows, (((1,), (1,)), ((), ())), preferred_element_type=jnp.float32
    )


def contract_first(left_rows, right_rows):
    return lax.dot_general(
        left_rows,
        right_rows,
        (((0,), (0,)), ((), ())),
        precision=highest,
        preferred_element_type=jnp.float32,
    )


def visibility(starts_row):
    seg_total = starts_row.shape[0]
    positions = jnp.arange(seg_total, dtype=jnp.int32)
    last_start = lax.cummax(jnp.where(starts_row == 1, positions, jnp.int32(-1)), axis=0)
    fresh_flag = (last_start < 0).astype(jnp.float32)
    seen_pairs = (
        (positions[:, None] >= last_start[None, :]) & (positions[:, None] < positions[None, :])
    ).astype(jnp.float32)
    seen_final = (positions >= last_start[seg_total - 1]).astype(jnp.float32)
    return (fresh_flag, seen_pairs, seen_final)


def normalized(rows, gain_row):
    wide = rows.astype(jnp.float32)
    inverse_rms = lax.rsqrt(jnp.mean(wide * wide, axis=-1, keepdims=True) + epsilon)
    return (wide * inverse_rms * gain_row.astype(jnp.float32)).astype(jnp.bfloat16)


def solved(mixing, initial):
    size = mixing.shape[0]
    power = -mixing.T
    writes = initial + jnp.dot(power, initial, precision=highest)
    span = 2
    while span < size // MEM:
        power = jnp.dot(power, power, precision=highest)
        writes = writes + jnp.dot(power, writes, precision=highest)
        span *= 2
    return writes


def rows_by_rows(left, right, precision=None):
    return lax.dot_general(
        left,
        right,
        (((1,), (1,)), ((), ())),
        precision=precision,
        preferred_element_type=jnp.float32,
    )


def phi(v):
    return jnp.where(v > 0, v + 1.0, jnp.exp(jnp.minimum(v, 0.0)))


def chain_kernel(
    leaving, w_query, w_key, w_value, w_gate, gain, matrix, totals_in, starts,
    updated, matrix_out, totals_out,
    mem_rows, rows, normed, wq, wk, wv, slots, memory, keys, writes, queries, base, stage, guests,
    final, matrix_new, sims,
    load_sem, shift_send, shift_recv, slot_send, slot_recv, mem_send, mem_recv, key_send, key_recv,
    write_send, write_recv, query_send, query_recv, base_send, base_recv, store_sem,
):
    seg = lax.axis_index("seg")
    section = lax.axis_index("section")
    sections = lax.axis_size("section")
    z = seg // 2
    core = seg % 2
    pair = z + 1 - 2 * (z % 2)
    inner = (z + 1) // 2 == 1
    outer = (z + 1) // 2 != 1
    middle = jnp.where(inner, 3 - z, 3 - pair)
    far = jnp.where(inner, 3 - pair, 3 - z)
    partner = 2 * z + 1 - core
    pair_seg = 2 * pair + core
    pair_cross = 2 * pair + 1 - core
    across_seg = 2 * (3 - z) + core
    after = (section + 1) % sections
    before = (section + sections - 1) % sections
    row_count = rows.shape[0]
    width = slots.shape[1]
    part = keys.shape[2]
    seg_count = keys.shape[0]
    mem_total = memory.shape[0]
    half = width // 2
    pieces = slot_send.shape[1]
    depth = width // pieces

    def remote(src, dst, send, recv, to_seg, to_section=section):
        return pltpu.make_async_remote_copy(
            src_ref=src, dst_ref=dst, send_sem=send, recv_sem=recv,
            device_id=(to_seg, to_section), device_id_type=pl.DeviceIdType.MESH,
        )

    loads = [
        pltpu.make_async_copy(w_key.at[0], wk, load_sem.at[0]),
        pltpu.make_async_copy(w_value.at[0], wv, load_sem.at[1]),
        pltpu.make_async_copy(matrix.at[0], slots.at[0], load_sem.at[2]),
        pltpu.make_async_copy(w_query.at[0], wq, load_sem.at[3]),
    ]
    for load in loads:
        load.start()

    barrier = pltpu.get_barrier_semaphore()
    for to_seg, to_section in (
        (seg, after), (seg, before), (partner, section), (pair_seg, section), (pair_cross, section)
    ):
        pl.semaphore_signal(
            barrier, inc=1, device_id=(to_seg, to_section), device_id_type=pl.DeviceIdType.MESH
        )

    @pl.when(inner)
    def _():
        pl.semaphore_signal(
            barrier, inc=1, device_id=(across_seg, section), device_id_type=pl.DeviceIdType.MESH
        )
        pl.semaphore_wait(barrier, 6)

    @pl.when(outer)
    def _():
        pl.semaphore_wait(barrier, 5)

    mem_shift = remote(
        leaving.at[0, 0, pl.ds(0, MEM)], mem_rows, shift_send.at[0], shift_recv.at[0], seg, after
    )
    mem_shift.start()
    cut = (row_count // 2 + 15) // 16 * 16
    bounds = ((0, cut), (cut, row_count))
    row_shift = []
    for n, (low, high) in enumerate(bounds):
        some = pl.ds(low, high - low)
        row_shift.append(
            remote(
                leaving.at[0, 0, some], rows.at[some], shift_send.at[1 + n],
                shift_recv.at[1 + n], seg, after,
            )
        )
        row_shift[n].start()

    def slot_copy(kind, piece):
        span = pl.ds(piece * depth, depth)
        source = slots.at[1, span] if kind == 3 else matrix.at[0, span]
        to_seg = pair_seg if kind == 1 else across_seg
        return remote(
            source, slots.at[kind, span], slot_send.at[kind - 1, piece],
            slot_recv.at[kind - 1, piece], to_seg,
        )

    def pump(first, last):
        for number in range(first, last):
            if number < pieces:
                @pl.when(outer)
                def _():
                    slot_copy(1, number).start()

                @pl.when(inner)
                def _():
                    slot_copy(2, number).start()
            else:
                @pl.when(inner)
                def _():
                    slot_copy(1, number - pieces).wait_recv()
                    slot_copy(3, number - pieces).start()

    pump(0, 1)

    same_core = [2 * chip + core for chip in (pair, middle, far)]
    other_core = [2 * chip + 1 - core for chip in (z, pair, middle, far)]

    def gather(view, send, recv):
        def copy(index, number, to_seg):
            return remote(view(index), view(index), send.at[number], recv.at[index], to_seg)

        def begin():
            copy(seg, 0, pair_seg).start()

            @pl.when(inner)
            def _():
                copy(seg, 1, across_seg).start()

            copy(seg, 2, partner).start()

        def relay(k):
            index = same_core[k]
            copy(index, 3 + k, partner).wait_recv()

            @pl.when(inner)
            def _():
                copy(index, 6 + k, across_seg if k == 0 else pair_seg).start()

            copy(index, 3 + k, partner).start()

        def arrive():
            for index in other_core:
                copy(index, 0, partner).wait_recv()

        def finish():
            copy(seg, 0, pair_seg).wait_send()
            copy(seg, 2, partner).wait_send()
            for k, index in enumerate(same_core):
                copy(index, 3 + k, partner).wait_send()

            @pl.when(inner)
            def _():
                copy(seg, 1, across_seg).wait_send()
                for k, index in enumerate(same_core):
                    copy(index, 6 + k, pair_seg).wait_send()

        return begin, relay, arrive, finish

    gain_row = gain[...].astype(jnp.float32)

    def normalize(some):
        wide = some.astype(jnp.float32)
        scale = lax.rsqrt(jnp.mean(wide * wide, axis=-1, keepdims=True) + epsilon)
        return (wide * scale * gain_row).astype(jnp.bfloat16)

    mem_begin, mem_relay, mem_arrive, mem_finish = gather(
        lambda index: memory.at[pl.ds(pl.multiple_of(index * MEM, MEM), MEM)], mem_send, mem_recv
    )
    mem_shift.wait_recv()
    memory[pl.ds(pl.multiple_of(seg * MEM, MEM), MEM), :] = normalize(mem_rows[...])
    mem_begin()
    for k in range(3):
        pump(1 + k, 2 + k)
        mem_relay(k)
    pump(4, 5)
    mem_arrive()

    key_begin, key_relay, key_arrive, key_finish = gather(
        lambda index: keys.at[index], key_send, key_recv
    )
    loads[0].wait()
    keys[seg] = phi(
        jnp.dot(memory[...], wk[...], preferred_element_type=jnp.float32)
    ).astype(jnp.bfloat16)
    key_begin()
    pump(5, 6)
    loads[1].wait()
    values = jnp.dot(memory[...], wv[...], preferred_element_type=jnp.float32)
    gate_logits = jnp.sum(
        memory[...].astype(jnp.float32) * w_gate[...].astype(jnp.float32), axis=-1, keepdims=True
    )
    rates = 1.0 / (1.0 + jnp.exp(-gate_logits))
    def query_copy(kind, n):
        low, high = bounds[n]
        span = pl.ds((2 * row_count if kind == 2 else 0) + low, high - low)
        landing = pl.ds((1 + kind) * row_count + low, high - low)
        return remote(
            queries.at[span], queries.at[landing], query_send.at[kind, n],
            query_recv.at[kind, n], pair_seg if kind == 1 else partner,
        )

    def make_queries(n):
        low, high = bounds[n]
        row_shift[n].wait_recv()

        @pl.loop(low // 16, high // 16)
        def _(step):
            some = pl.ds(pl.multiple_of(step * 16, 16), 16)
            normed[some, :] = normalize(rows[some, :])

        if n == 0:
            loads[3].wait()

        @pl.loop(0, seg_count)
        def _(b):
            cols = pl.ds(pl.multiple_of(b * part, part), part)
            queries[low:high, cols] = phi(
                jnp.dot(normed[low:high, :], wq[:, cols], preferred_element_type=jnp.float32)
            ).astype(jnp.bfloat16)

        @pl.when(outer)
        def _():
            query_copy(1, n).start()

        query_copy(0, n).start()

    def pass_guests(n):
        @pl.when(inner)
        def _():
            query_copy(1, n).wait_recv()
            query_copy(2, n).start()

    pump(6, 8)
    make_queries(0)
    for k in range(3):
        key_relay(k)
        pump(8 + k, 9 + k)
    key_arrive()
    pump(11, 12)

    def last_start(positions):
        last = jnp.full(positions.shape, -1, jnp.int32)
        for j in range(seg_count):
            last = jnp.maximum(last, jnp.where((starts[0, j] == 1) & (positions >= j), j, -1))
        return last

    square = (mem_total, mem_total)
    to_segment = lax.broadcasted_iota(jnp.int32, square, 0) // MEM
    from_segment = lax.broadcasted_iota(jnp.int32, square, 1) // MEM
    seen = ((from_segment >= last_start(to_segment)) & (from_segment < to_segment)).astype(
        jnp.float32
    )
    row_segment = lax.broadcasted_iota(jnp.int32, (mem_total, 1), 0) // MEM
    fresh_rows = (last_start(row_segment) < 0).astype(jnp.float32)
    final_segment = jnp.full((mem_total, 1), seg_count - 1, jnp.int32)
    end_last = last_start(final_segment)
    end_rows = (row_segment >= end_last).astype(jnp.float32)
    fresh_end = (end_last[:1] < 0).astype(jnp.float32)

    loads[2].wait()
    gram = jnp.zeros(square, jnp.float32)
    probed = jnp.zeros((mem_total, width), jnp.float32)
    start_scale = jnp.zeros((mem_total, 1), jnp.float32)
    for b in range(seg_count):
        cols = pl.ds(b * part, part)
        block = keys[b]
        gram += rows_by_rows(block, block)
        probed += rows_by_rows(block, slots[0, :, cols])
        start_scale += jnp.sum(
            block.astype(jnp.float32) * totals_in[:, cols], axis=-1, keepdims=True
        )
    visible = seen * gram
    scales = jnp.maximum(
        fresh_rows * start_scale + jnp.sum(visible, axis=-1, keepdims=True), 1.0
    )
    power = -(rates / scales) * visible
    solved_rows = rates * (values - (fresh_rows / scales) * probed)
    span = 1
    while span < seg_count:
        solved_rows += jnp.dot(
            power, solved_rows, precision=highest, preferred_element_type=jnp.float32
        )
        span *= 2
        if span < seg_count:
            power = jnp.dot(power, power, precision=highest, preferred_element_type=jnp.float32)
    write_begin, write_relay, write_arrive, write_finish = gather(
        lambda index: writes.at[index], write_send, write_recv
    )
    writes[seg] = solved_rows.astype(jnp.bfloat16)
    write_begin()

    pump(12, 14)
    make_queries(1)
    pump(14, 2 * pieces)
    pass_guests(0)

    key_segment = lax.broadcasted_iota(jnp.int32, (1, mem_total), 1) // MEM
    my_segment = jnp.full((1, mem_total), 0, jnp.int32) + seg
    my_last = last_start(my_segment)
    my_mask = ((key_segment >= my_last) & (key_segment < my_segment)).astype(jnp.float32)
    my_fresh = (my_last[:, :1] < 0).astype(jnp.float32)
    similarity = jnp.zeros((row_count, mem_total), jnp.float32)
    query_scale = jnp.zeros((row_count, 1), jnp.float32)
    for b in range(seg_count):
        cols = pl.ds(b * part, part)
        mine = queries[:row_count, cols]
        similarity += rows_by_rows(mine, keys[b])
        query_scale += jnp.sum(
            mine.astype(jnp.float32) * totals_in[:, cols], axis=-1, keepdims=True
        )
    similarity *= my_mask
    inverse = 1.0 / jnp.maximum(
        my_fresh * query_scale + jnp.sum(similarity, axis=-1, keepdims=True), 1.0
    )
    sims[...] = similarity.astype(jnp.bfloat16)
    my_scale = my_fresh * inverse

    write_relay(0)

    ended = (solved_rows * end_rows).T
    for b in range(seg_count):
        cols = pl.ds(b * part, part)
        block = keys[b].astype(jnp.float32)
        matrix_new[:, cols] = (
            fresh_end * slots[0, :, cols].astype(jnp.float32)
            + jnp.dot(ended, block, precision=highest, preferred_element_type=jnp.float32)
        ).astype(jnp.bfloat16)
        totals_out[:, cols] = fresh_end * totals_in[:, cols] + jnp.sum(
            end_rows * block, axis=0, keepdims=True
        )
    matrix_store = pltpu.make_async_copy(matrix_new, matrix_out.at[0], store_sem.at[0])
    matrix_store.start()

    write_relay(1)

    def partner_copy(slot, column):
        return remote(
            stage.at[slot], base.at[column], base_send.at[slot], base_recv.at[column, 0], partner
        )

    def partner_half(h, column):
        cols = pl.ds(h * half, half)
        return remote(
            stage.at[3, :, cols], base.at[column, :, cols], base_send.at[10 + h],
            base_recv.at[column, h], partner,
        )

    guest_slots = (0, 2)

    def guest_copy(number, which, column):
        return remote(
            guests.at[2 * number + which], base.at[column], base_send.at[4 + 2 * number + which],
            base_recv.at[column, 0], pair_cross if which else pair_seg,
        )

    def guest_half(h, which, column):
        cols = pl.ds(h * half, half)
        return remote(
            guests.at[4 + which, :, cols], base.at[column, :, cols],
            base_send.at[12 + 2 * h + which], base_recv.at[column, h],
            pair_cross if which else pair_seg,
        )

    def far_read(h, column):
        cols = pl.ds(h * half, half)
        for piece in range(h * pieces // 2, (h + 1) * pieces // 2):
            slot_copy(3, piece).wait_recv()
        part_read = rows_by_rows(queries[...], slots[3, pl.ds(h * half, half)]).astype(
            jnp.bfloat16
        )
        for which in range(2):
            guests[4 + which, :, cols] = part_read[
                (2 + which) * row_count : (3 + which) * row_count
            ]
            guest_half(h, which, column).start()
        stage[3, :, cols] = part_read[row_count : 2 * row_count]
        partner_half(h, column).start()
        base[column, :, cols] = part_read[:row_count]

    def chip_read(slot, column):
        part_read = rows_by_rows(queries[: 2 * row_count], slots[slot]).astype(jnp.bfloat16)
        stage[slot] = part_read[row_count:]
        partner_copy(slot, column).start()
        base[column] = part_read[:row_count]

    def guest_read(number, column):
        part_read = rows_by_rows(
            queries[2 * row_count :], slots[guest_slots[number]]
        ).astype(jnp.bfloat16)
        for which in range(2):
            guests[2 * number + which] = part_read[which * row_count : (1 + which) * row_count]
            guest_copy(number, which, column).start()

    for n in range(2):
        query_copy(0, n).wait_recv()
    chip_read(0, seg)
    write_relay(2)
    pass_guests(1)

    @pl.when(inner)
    def _():
        chip_read(1, same_core[0])
        for n in range(2):
            query_copy(2, n).wait_recv()
        guest_read(0, seg)
        for piece in range(pieces):
            slot_copy(2, piece).wait_recv()
        guest_read(1, same_core[1])
        chip_read(2, same_core[1])

    write_arrive()

    def combine(column):
        cols = pl.ds(pl.multiple_of(column * width, width), width)
        low = jnp.dot(sims[...], writes[column], preferred_element_type=jnp.float32)
        final[:, cols] = (
            rows[:, cols].astype(jnp.float32)
            + my_scale * base[column].astype(jnp.float32)
            + inverse * low
        ).astype(jnp.bfloat16)
        return pltpu.make_async_copy(
            final.at[:, cols], updated.at[0, 0, :, cols], store_sem.at[1 + column]
        )

    stores = [combine(seg)]
    stores[0].start()

    def landed(column, halves=False):
        if halves:
            partner_half(0, column).wait_recv()
            partner_half(1, column).wait_recv()
        else:
            partner_copy(0, column).wait_recv()

    landed(partner)
    stores.append(combine(partner))
    stores[-1].start()
    for k in range(3):
        if k == 2:
            @pl.when(inner)
            def _():
                far_read(0, same_core[2])
                far_read(1, same_core[2])

        @pl.when(outer)
        def _():
            landed(same_core[k], k == 2)

        stores.append(combine(same_core[k]))
        stores[-1].start()
        landed(other_core[k + 1], k == 2)
        stores.append(combine(other_core[k + 1]))
        stores[-1].start()

    mem_shift.wait_send()
    for n in range(2):
        row_shift[n].wait_send()
        query_copy(0, n).wait_send()
    partner_copy(0, seg).wait_send()

    @pl.when(outer)
    def _():
        for piece in range(pieces):
            slot_copy(1, piece).wait_send()
        for n in range(2):
            query_copy(1, n).wait_send()

    @pl.when(inner)
    def _():
        for piece in range(pieces):
            slot_copy(2, piece).wait_send()
            slot_copy(3, piece).wait_send()
        for n in range(2):
            query_copy(2, n).wait_send()
        for slot in (1, 2):
            partner_copy(slot, seg).wait_send()
        for which in range(2):
            for number in range(2):
                guest_copy(number, which, seg).wait_send()
            partner_half(which, seg).wait_send()
            for h in range(2):
                guest_half(h, which, seg).wait_send()

    mem_finish()
    key_finish()
    write_finish()
    matrix_store.wait()
    for store in stores:
        store.wait()


def chained(
    leaving, w_query, w_key, w_value, w_gate, norm_gain, memory_matrix, key_totals, doc_starts
):
    seg_count = lax.axis_size("seg")
    rows, features = leaving.shape[2:]
    key_width = w_query.shape[2]
    part = w_key.shape[2]
    width = memory_matrix.shape[1]
    mem_total = seg_count * MEM
    short = jnp.bfloat16
    anywhere = pl.BlockSpec(memory_space=pl.ANY)
    near = pl.BlockSpec(memory_space=pltpu.VMEM)
    dma = pltpu.SemaphoreType.DMA
    updated, matrix_next, totals_next = pl.pallas_call(
        chain_kernel,
        out_shape=(
            jax.ShapeDtypeStruct(leaving.shape, short),
            jax.ShapeDtypeStruct(memory_matrix.shape, short),
            jax.ShapeDtypeStruct(key_totals.shape, jnp.float32),
        ),
        in_specs=[
            anywhere, anywhere, anywhere, anywhere, near, near, anywhere, near,
            pl.BlockSpec(memory_space=pltpu.SMEM),
        ],
        out_specs=(anywhere, anywhere, near),
        scratch_shapes=[
            pltpu.VMEM((MEM, features), short),
            pltpu.VMEM((rows, features), short),
            pltpu.VMEM((rows, features), short),
            pltpu.VMEM((features, key_width), short),
            pltpu.VMEM((features, part), short),
            pltpu.VMEM((features, width), short),
            pltpu.VMEM((4, width, key_width), short),
            pltpu.VMEM((mem_total, features), short),
            pltpu.VMEM((seg_count, mem_total, part), short),
            pltpu.VMEM((seg_count, mem_total, width), short),
            pltpu.VMEM((4 * rows, key_width), short),
            pltpu.VMEM((seg_count, rows, width), short),
            pltpu.VMEM((4, rows, width), short),
            pltpu.VMEM((6, rows, width), short),
            pltpu.VMEM((rows, features), short),
            pltpu.VMEM((width, key_width), short),
            pltpu.VMEM((rows, mem_total), short),
            dma((4,)), dma((3,)), dma((3,)), dma((3, 8)), dma((3, 8)),
            dma((9,)), dma((seg_count,)), dma((9,)), dma((seg_count,)),
            dma((9,)), dma((seg_count,)), dma((3, 2)), dma((3, 2)),
            dma((16,)), dma((seg_count, 2)), dma((1 + seg_count,)),
        ],
        compiler_params=pltpu.CompilerParams(
            collective_id=0, has_side_effects=True, vmem_limit_bytes=63 * 1024 * 1024
        ),
    )(
        leaving, w_query, w_key, w_value, w_gate, norm_gain, memory_matrix, key_totals, doc_starts
    )
    return (updated, matrix_next, totals_next)


def local(
    leaving, w_query, w_key, w_value, w_gate, norm_gain, memory_matrix, key_totals, doc_starts
):
    seg_count = lax.axis_size("seg")
    my_index = lax.axis_index("seg")
    memory_rows = shifted(leaving[0, 0, :MEM], "section", 1)
    entering = shifted(leaving, "section", 1)[0, 0]
    matrix = memory_matrix[0]
    whole_matrix = lax.all_gather(matrix, "seg", axis=0, tiled=True)
    memory = lax.all_gather(normalized(memory_rows, norm_gain[0]), "seg", axis=0, tiled=True)
    key_part = feature_map(jnp.dot(memory, w_key[0], preferred_element_type=jnp.float32)).astype(
        jnp.bfloat16
    )
    value_part = jnp.dot(memory, w_value[0], preferred_element_type=jnp.float32)
    gate_rates = jax.nn.sigmoid(jnp.dot(memory, w_gate[0], preferred_element_type=jnp.float32))
    key_rows = lax.all_gather(key_part, "seg", axis=1, tiled=True)
    fresh_flag, seen_pairs, seen_final = visibility(doc_starts[0])
    key_wide = key_rows.astype(jnp.float32)
    key_sums = key_wide.reshape(seg_count, MEM, -1).sum(axis=1)
    totals = fresh_flag[:, None] * key_totals[0][None, :] + jnp.dot(
        seen_pairs.T, key_sums, precision=highest
    )
    total_rows = jnp.repeat(totals, MEM, axis=0)
    key_scales = jnp.maximum(jnp.sum(total_rows * key_wide, axis=-1), 1.0)
    key_gram = contract_last(key_rows, key_rows)
    seen_cols = jnp.repeat(jnp.repeat(seen_pairs, MEM, axis=0), MEM, axis=1)
    mixing = seen_cols * key_gram * (gate_rates / key_scales)[None, :]
    fresh_rows = jnp.repeat(fresh_flag, MEM)
    probed_keys = contract_last(key_rows, matrix)
    initial = gate_rates[:, None] * (
        value_part - (fresh_rows / key_scales)[:, None] * probed_keys
    )
    write_cols = solved(mixing, initial)
    writes = lax.all_gather(write_cols.astype(jnp.bfloat16), "seg", axis=1, tiled=True)
    fresh_end = fresh_flag[seg_count - 1]
    end_rows = jnp.repeat(seen_final, MEM)
    matrix_next = (
        fresh_end * matrix.astype(jnp.float32)
        + contract_first(write_cols * end_rows[:, None], key_wide)
    ).astype(jnp.bfloat16)
    totals_next = fresh_end * key_totals[0] + jnp.dot(seen_final, key_sums, precision=highest)
    normed = normalized(entering, norm_gain[0])
    queries = feature_map(jnp.dot(normed, w_query[0], preferred_element_type=jnp.float32)).astype(
        jnp.bfloat16
    )
    my_fresh = fresh_flag[my_index]
    column_mask = jnp.repeat(seen_pairs[:, my_index], MEM)
    my_totals = lax.dynamic_slice_in_dim(totals, my_index, 1, 0)
    denominator = jnp.maximum(jnp.sum(queries.astype(jnp.float32) * my_totals, axis=-1), 1.0)
    similarity = contract_last(queries, key_rows) * column_mask[None, :]
    low_rank = jnp.dot(
        similarity.astype(jnp.bfloat16), writes, preferred_element_type=jnp.float32
    )
    base_read = contract_last(queries, whole_matrix)
    updated = (
        entering.astype(jnp.float32) + (my_fresh * base_read + low_rank) / denominator[:, None]
    ).astype(jnp.bfloat16)
    return (updated[None, None], matrix_next[None], totals_next[None])


def solution(mesh):
    fits = mesh.shape["seg"] == 8 and mesh.shape["section"] > 2
    return jax.shard_map(
        chained if fits else local,
        mesh=mesh,
        in_specs=(
            P("seg", "section", None, None),
            P("section", None, None),
            P("section", None, "seg"),
            P("section", None, "seg"),
            P("section", None),
            P("section", None),
            P("section", "seg", None),
            P("section", None),
            P("section", None),
        ),
        out_specs=(P("seg", "section", None, None), P("section", "seg", None), P("section", None)),
        check_vma=False,
    )
```

```python
import jax
import jax.numpy as jnp
from jax import lax
from jax.experimental import pallas as pl
from jax.experimental.pallas import tpu as pltpu
from jax.sharding import PartitionSpec as P

MEM = 16


highest = lax.Precision.HIGHEST
epsilon = 1e-05


def shifted(shard, axis, by):
    size = lax.axis_size(axis)
    return lax.ppermute(shard, axis, [(i, (i + by) % size) for i in range(size)])


def feature_map(projected):
    return jax.nn.elu(projected) + 1.0


def contract_last(left_rows, right_rows):
    return lax.dot_general(
        left_rows, right_rows, (((1,), (1,)), ((), ())), preferred_element_type=jnp.float32
    )


def contract_first(left_rows, right_rows):
    return lax.dot_general(
        left_rows,
        right_rows,
        (((0,), (0,)), ((), ())),
        precision=highest,
        preferred_element_type=jnp.float32,
    )


def visibility(starts_row):
    seg_total = starts_row.shape[0]
    positions = jnp.arange(seg_total, dtype=jnp.int32)
    last_start = lax.cummax(jnp.where(starts_row == 1, positions, jnp.int32(-1)), axis=0)
    fresh_flag = (last_start < 0).astype(jnp.float32)
    seen_pairs = (
        (positions[:, None] >= last_start[None, :]) & (positions[:, None] < positions[None, :])
    ).astype(jnp.float32)
    seen_final = (positions >= last_start[seg_total - 1]).astype(jnp.float32)
    return (fresh_flag, seen_pairs, seen_final)


def normalized(rows, gain_row):
    wide = rows.astype(jnp.float32)
    inverse_rms = lax.rsqrt(jnp.mean(wide * wide, axis=-1, keepdims=True) + epsilon)
    return (wide * inverse_rms * gain_row.astype(jnp.float32)).astype(jnp.bfloat16)


def solved(mixing, initial):
    size = mixing.shape[0]
    power = -mixing.T
    writes = initial + jnp.dot(power, initial, precision=highest)
    span = 2
    while span < size // MEM:
        power = jnp.dot(power, power, precision=highest)
        writes = writes + jnp.dot(power, writes, precision=highest)
        span *= 2
    return writes


def rows_by_rows(left, right, precision=None):
    return lax.dot_general(
        left,
        right,
        (((1,), (1,)), ((), ())),
        precision=precision,
        preferred_element_type=jnp.float32,
    )


def phi(v):
    return jnp.where(v > 0, v + 1.0, jnp.exp(jnp.minimum(v, 0.0)))


def chain_kernel(
    leaving, w_query, w_key, w_value, w_gate, gain, matrix, totals_in, starts,
    updated, matrix_out, totals_out,
    mem_rows, rows, normed, wq, wk, wv, slots, memory, keys, writes, queries, base, stage, guests,
    final, matrix_new, sims,
    load_sem, shift_send, shift_recv, slot_send, slot_recv, mem_send, mem_recv, key_send, key_recv,
    write_send, write_recv, query_send, query_recv, base_send, base_recv, store_sem,
):
    seg = lax.axis_index("seg")
    section = lax.axis_index("section")
    sections = lax.axis_size("section")
    z = seg // 2
    core = seg % 2
    pair = z + 1 - 2 * (z % 2)
    inner = (z + 1) // 2 == 1
    outer = (z + 1) // 2 != 1
    middle = jnp.where(inner, 3 - z, 3 - pair)
    far = jnp.where(inner, 3 - pair, 3 - z)
    partner = 2 * z + 1 - core
    pair_seg = 2 * pair + core
    pair_cross = 2 * pair + 1 - core
    across_seg = 2 * (3 - z) + core
    after = (section + 1) % sections
    before = (section + sections - 1) % sections
    row_count = rows.shape[0]
    width = slots.shape[1]
    part = keys.shape[2]
    seg_count = keys.shape[0]
    mem_total = memory.shape[0]
    half = width // 2
    pieces = slot_send.shape[1]
    depth = width // pieces

    def remote(src, dst, send, recv, to_seg, to_section=section):
        return pltpu.make_async_remote_copy(
            src_ref=src, dst_ref=dst, send_sem=send, recv_sem=recv,
            device_id=(to_seg, to_section), device_id_type=pl.DeviceIdType.MESH,
        )

    loads = [
        pltpu.make_async_copy(w_key.at[0], wk, load_sem.at[0]),
        pltpu.make_async_copy(w_value.at[0], wv, load_sem.at[1]),
        pltpu.make_async_copy(matrix.at[0], slots.at[0], load_sem.at[2]),
        pltpu.make_async_copy(w_query.at[0], wq, load_sem.at[3]),
    ]
    for load in loads:
        load.start()

    barrier = pltpu.get_barrier_semaphore()
    for to_seg, to_section in (
        (seg, after), (seg, before), (partner, section), (pair_seg, section), (pair_cross, section)
    ):
        pl.semaphore_signal(
            barrier, inc=1, device_id=(to_seg, to_section), device_id_type=pl.DeviceIdType.MESH
        )

    @pl.when(inner)
    def _():
        pl.semaphore_signal(
            barrier, inc=1, device_id=(across_seg, section), device_id_type=pl.DeviceIdType.MESH
        )
        pl.semaphore_wait(barrier, 6)

    @pl.when(outer)
    def _():
        pl.semaphore_wait(barrier, 5)

    mem_shift = remote(
        leaving.at[0, 0, pl.ds(0, MEM)], mem_rows, shift_send.at[0], shift_recv.at[0], seg, after
    )
    mem_shift.start()
    cut = (row_count // 2 + 15) // 16 * 16
    bounds = ((0, cut), (cut, row_count))
    row_shift = []
    for n, (low, high) in enumerate(bounds):
        some = pl.ds(low, high - low)
        row_shift.append(
            remote(
                leaving.at[0, 0, some], rows.at[some], shift_send.at[1 + n],
                shift_recv.at[1 + n], seg, after,
            )
        )
        row_shift[n].start()

    def slot_copy(kind, piece):
        span = pl.ds(piece * depth, depth)
        source = slots.at[1, span] if kind == 3 else matrix.at[0, span]
        to_seg = pair_seg if kind == 1 else across_seg
        return remote(
            source, slots.at[kind, span], slot_send.at[kind - 1, piece],
            slot_recv.at[kind - 1, piece], to_seg,
        )

    def pump(first, last):
        for number in range(first, last):
            if number < pieces:
                @pl.when(outer)
                def _():
                    slot_copy(1, number).start()

                @pl.when(inner)
                def _():
                    slot_copy(2, number).start()
            else:
                @pl.when(inner)
                def _():
                    slot_copy(1, number - pieces).wait_recv()
                    slot_copy(3, number - pieces).start()

    pump(0, 1)

    same_core = [2 * chip + core for chip in (pair, middle, far)]
    other_core = [2 * chip + 1 - core for chip in (z, pair, middle, far)]

    def gather(view, send, recv):
        def copy(index, number, to_seg):
            return remote(view(index), view(index), send.at[number], recv.at[index], to_seg)

        def begin():
            copy(seg, 0, pair_seg).start()

            @pl.when(inner)
            def _():
                copy(seg, 1, across_seg).start()

            copy(seg, 2, partner).start()

        def relay(k):
            index = same_core[k]
            copy(index, 3 + k, partner).wait_recv()

            @pl.when(inner)
            def _():
                copy(index, 6 + k, across_seg if k == 0 else pair_seg).start()

            copy(index, 3 + k, partner).start()

        def arrive():
            for index in other_core:
                copy(index, 0, partner).wait_recv()

        def finish():
            copy(seg, 0, pair_seg).wait_send()
            copy(seg, 2, partner).wait_send()
            for k, index in enumerate(same_core):
                copy(index, 3 + k, partner).wait_send()

            @pl.when(inner)
            def _():
                copy(seg, 1, across_seg).wait_send()
                for k, index in enumerate(same_core):
                    copy(index, 6 + k, pair_seg).wait_send()

        return begin, relay, arrive, finish

    gain_row = gain[...].astype(jnp.float32)

    def normalize(some):
        wide = some.astype(jnp.float32)
        scale = lax.rsqrt(jnp.mean(wide * wide, axis=-1, keepdims=True) + epsilon)
        return (wide * scale * gain_row).astype(jnp.bfloat16)

    mem_begin, mem_relay, mem_arrive, mem_finish = gather(
        lambda index: memory.at[pl.ds(pl.multiple_of(index * MEM, MEM), MEM)], mem_send, mem_recv
    )
    mem_shift.wait_recv()
    memory[pl.ds(pl.multiple_of(seg * MEM, MEM), MEM), :] = normalize(mem_rows[...])
    mem_begin()
    for k in range(3):
        pump(1 + k, 2 + k)
        mem_relay(k)
    pump(4, 5)
    mem_arrive()

    key_begin, key_relay, key_arrive, key_finish = gather(
        lambda index: keys.at[index], key_send, key_recv
    )
    loads[0].wait()
    keys[seg] = phi(
        jnp.dot(memory[...], wk[...], preferred_element_type=jnp.float32)
    ).astype(jnp.bfloat16)
    key_begin()
    pump(5, 6)
    loads[1].wait()
    values = jnp.dot(memory[...], wv[...], preferred_element_type=jnp.float32)
    gate_logits = jnp.sum(
        memory[...].astype(jnp.float32) * w_gate[...].astype(jnp.float32), axis=-1, keepdims=True
    )
    rates = 1.0 / (1.0 + jnp.exp(-gate_logits))
    def query_copy(kind, n):
        low, high = bounds[n]
        span = pl.ds((2 * row_count if kind == 2 else 0) + low, high - low)
        landing = pl.ds((1 + kind) * row_count + low, high - low)
        return remote(
            queries.at[span], queries.at[landing], query_send.at[kind, n],
            query_recv.at[kind, n], pair_seg if kind == 1 else partner,
        )

    def make_queries(n):
        low, high = bounds[n]
        row_shift[n].wait_recv()

        @pl.loop(low // 16, high // 16)
        def _(step):
            some = pl.ds(pl.multiple_of(step * 16, 16), 16)
            normed[some, :] = normalize(rows[some, :])

        if n == 0:
            loads[3].wait()

        @pl.loop(0, seg_count)
        def _(b):
            cols = pl.ds(pl.multiple_of(b * part, part), part)
            queries[low:high, cols] = phi(
                jnp.dot(normed[low:high, :], wq[:, cols], preferred_element_type=jnp.float32)
            ).astype(jnp.bfloat16)

        @pl.when(outer)
        def _():
            query_copy(1, n).start()

        query_copy(0, n).start()

    def pass_guests(n):
        @pl.when(inner)
        def _():
            query_copy(1, n).wait_recv()
            query_copy(2, n).start()

    for k in range(3):
        key_relay(k)
        pump(6 + k, 7 + k)
    key_arrive()
    pump(9, 10)

    def last_start(positions):
        last = jnp.full(positions.shape, -1, jnp.int32)
        for j in range(seg_count):
            last = jnp.maximum(last, jnp.where((starts[0, j] == 1) & (positions >= j), j, -1))
        return last

    square = (mem_total, mem_total)
    to_segment = lax.broadcasted_iota(jnp.int32, square, 0) // MEM
    from_segment = lax.broadcasted_iota(jnp.int32, square, 1) // MEM
    seen = ((from_segment >= last_start(to_segment)) & (from_segment < to_segment)).astype(
        jnp.float32
    )
    row_segment = lax.broadcasted_iota(jnp.int32, (mem_total, 1), 0) // MEM
    fresh_rows = (last_start(row_segment) < 0).astype(jnp.float32)
    final_segment = jnp.full((mem_total, 1), seg_count - 1, jnp.int32)
    end_last = last_start(final_segment)
    end_rows = (row_segment >= end_last).astype(jnp.float32)
    fresh_end = (end_last[:1] < 0).astype(jnp.float32)

    loads[2].wait()
    gram = jnp.zeros(square, jnp.float32)
    probed = jnp.zeros((mem_total, width), jnp.float32)
    start_scale = jnp.zeros((mem_total, 1), jnp.float32)
    for b in range(seg_count):
        cols = pl.ds(b * part, part)
        block = keys[b]
        gram += rows_by_rows(block, block)
        probed += rows_by_rows(block, slots[0, :, cols])
        start_scale += jnp.sum(
            block.astype(jnp.float32) * totals_in[:, cols], axis=-1, keepdims=True
        )
    visible = seen * gram
    scales = jnp.maximum(
        fresh_rows * start_scale + jnp.sum(visible, axis=-1, keepdims=True), 1.0
    )
    power = -(rates / scales) * visible
    solved_rows = rates * (values - (fresh_rows / scales) * probed)
    span = 1
    while span < seg_count:
        solved_rows += jnp.dot(
            power, solved_rows, precision=highest, preferred_element_type=jnp.float32
        )
        span *= 2
        if span < seg_count:
            power = jnp.dot(power, power, precision=highest, preferred_element_type=jnp.float32)
    write_begin, write_relay, write_arrive, write_finish = gather(
        lambda index: writes.at[index], write_send, write_recv
    )
    writes[seg] = solved_rows.astype(jnp.bfloat16)
    write_begin()

    pump(10, 11)
    make_queries(0)
    for k in range(3):
        write_relay(k)
        pump(11 + k, 12 + k)
    pump(14, 2 * pieces)
    make_queries(1)
    pass_guests(0)

    key_segment = lax.broadcasted_iota(jnp.int32, (1, mem_total), 1) // MEM
    my_segment = jnp.full((1, mem_total), 0, jnp.int32) + seg
    my_last = last_start(my_segment)
    my_mask = ((key_segment >= my_last) & (key_segment < my_segment)).astype(jnp.float32)
    my_fresh = (my_last[:, :1] < 0).astype(jnp.float32)
    similarity = jnp.zeros((row_count, mem_total), jnp.float32)
    query_scale = jnp.zeros((row_count, 1), jnp.float32)
    for b in range(seg_count):
        cols = pl.ds(b * part, part)
        mine = queries[:row_count, cols]
        similarity += rows_by_rows(mine, keys[b])
        query_scale += jnp.sum(
            mine.astype(jnp.float32) * totals_in[:, cols], axis=-1, keepdims=True
        )
    similarity *= my_mask
    inverse = 1.0 / jnp.maximum(
        my_fresh * query_scale + jnp.sum(similarity, axis=-1, keepdims=True), 1.0
    )
    sims[...] = similarity.astype(jnp.bfloat16)
    my_scale = my_fresh * inverse

    ended = (solved_rows * end_rows).T
    for b in range(seg_count):
        cols = pl.ds(b * part, part)
        block = keys[b].astype(jnp.float32)
        matrix_new[:, cols] = (
            fresh_end * slots[0, :, cols].astype(jnp.float32)
            + jnp.dot(ended, block, precision=highest, preferred_element_type=jnp.float32)
        ).astype(jnp.bfloat16)
        totals_out[:, cols] = fresh_end * totals_in[:, cols] + jnp.sum(
            end_rows * block, axis=0, keepdims=True
        )
    matrix_store = pltpu.make_async_copy(matrix_new, matrix_out.at[0], store_sem.at[0])
    matrix_store.start()

    def partner_copy(slot, column):
        return remote(
            stage.at[slot], base.at[column], base_send.at[slot], base_recv.at[column, 0], partner
        )

    def partner_half(h, column):
        cols = pl.ds(h * half, half)
        return remote(
            stage.at[3, :, cols], base.at[column, :, cols], base_send.at[10 + h],
            base_recv.at[column, h], partner,
        )

    guest_slots = (0, 2)

    def guest_copy(number, which, column):
        return remote(
            guests.at[2 * number + which], base.at[column], base_send.at[4 + 2 * number + which],
            base_recv.at[column, 0], pair_cross if which else pair_seg,
        )

    def guest_half(h, which, column):
        cols = pl.ds(h * half, half)
        return remote(
            guests.at[4 + which, :, cols], base.at[column, :, cols],
            base_send.at[12 + 2 * h + which], base_recv.at[column, h],
            pair_cross if which else pair_seg,
        )

    def far_read(h, column):
        cols = pl.ds(h * half, half)
        for piece in range(h * pieces // 2, (h + 1) * pieces // 2):
            slot_copy(3, piece).wait_recv()
        part_read = rows_by_rows(queries[...], slots[3, pl.ds(h * half, half)]).astype(
            jnp.bfloat16
        )
        for which in range(2):
            guests[4 + which, :, cols] = part_read[
                (2 + which) * row_count : (3 + which) * row_count
            ]
            guest_half(h, which, column).start()
        stage[3, :, cols] = part_read[row_count : 2 * row_count]
        partner_half(h, column).start()
        base[column, :, cols] = part_read[:row_count]

    def chip_read(slot, column):
        part_read = rows_by_rows(queries[: 2 * row_count], slots[slot]).astype(jnp.bfloat16)
        stage[slot] = part_read[row_count:]
        partner_copy(slot, column).start()
        base[column] = part_read[:row_count]

    def guest_read(number, column):
        part_read = rows_by_rows(
            queries[2 * row_count :], slots[guest_slots[number]]
        ).astype(jnp.bfloat16)
        for which in range(2):
            guests[2 * number + which] = part_read[which * row_count : (1 + which) * row_count]
            guest_copy(number, which, column).start()

    for n in range(2):
        query_copy(0, n).wait_recv()
    chip_read(0, seg)
    pass_guests(1)

    @pl.when(inner)
    def _():
        chip_read(1, same_core[0])
        for n in range(2):
            query_copy(2, n).wait_recv()
        guest_read(0, seg)
        for piece in range(pieces):
            slot_copy(2, piece).wait_recv()
        guest_read(1, same_core[1])
        chip_read(2, same_core[1])

    write_arrive()

    def combine(column):
        cols = pl.ds(pl.multiple_of(column * width, width), width)
        low = jnp.dot(sims[...], writes[column], preferred_element_type=jnp.float32)
        final[:, cols] = (
            rows[:, cols].astype(jnp.float32)
            + my_scale * base[column].astype(jnp.float32)
            + inverse * low
        ).astype(jnp.bfloat16)
        return pltpu.make_async_copy(
            final.at[:, cols], updated.at[0, 0, :, cols], store_sem.at[1 + column]
        )

    stores = [combine(seg)]
    stores[0].start()

    def landed(column, halves=False):
        if halves:
            partner_half(0, column).wait_recv()
            partner_half(1, column).wait_recv()
        else:
            partner_copy(0, column).wait_recv()

    landed(partner)
    stores.append(combine(partner))
    stores[-1].start()
    for k in range(3):
        if k == 2:
            @pl.when(inner)
            def _():
                far_read(0, same_core[2])
                far_read(1, same_core[2])

        @pl.when(outer)
        def _():
            landed(same_core[k], k == 2)

        stores.append(combine(same_core[k]))
        stores[-1].start()
        landed(other_core[k + 1], k == 2)
        stores.append(combine(other_core[k + 1]))
        stores[-1].start()

    mem_shift.wait_send()
    for n in range(2):
        row_shift[n].wait_send()
        query_copy(0, n).wait_send()
    partner_copy(0, seg).wait_send()

    @pl.when(outer)
    def _():
        for piece in range(pieces):
            slot_copy(1, piece).wait_send()
        for n in range(2):
            query_copy(1, n).wait_send()

    @pl.when(inner)
    def _():
        for piece in range(pieces):
            slot_copy(2, piece).wait_send()
            slot_copy(3, piece).wait_send()
        for n in range(2):
            query_copy(2, n).wait_send()
        for slot in (1, 2):
            partner_copy(slot, seg).wait_send()
        for which in range(2):
            for number in range(2):
                guest_copy(number, which, seg).wait_send()
            partner_half(which, seg).wait_send()
            for h in range(2):
                guest_half(h, which, seg).wait_send()

    mem_finish()
    key_finish()
    write_finish()
    matrix_store.wait()
    for store in stores:
        store.wait()


def chained(
    leaving, w_query, w_key, w_value, w_gate, norm_gain, memory_matrix, key_totals, doc_starts
):
    seg_count = lax.axis_size("seg")
    rows, features = leaving.shape[2:]
    key_width = w_query.shape[2]
    part = w_key.shape[2]
    width = memory_matrix.shape[1]
    mem_total = seg_count * MEM
    short = jnp.bfloat16
    anywhere = pl.BlockSpec(memory_space=pl.ANY)
    near = pl.BlockSpec(memory_space=pltpu.VMEM)
    dma = pltpu.SemaphoreType.DMA
    updated, matrix_next, totals_next = pl.pallas_call(
        chain_kernel,
        out_shape=(
            jax.ShapeDtypeStruct(leaving.shape, short),
            jax.ShapeDtypeStruct(memory_matrix.shape, short),
            jax.ShapeDtypeStruct(key_totals.shape, jnp.float32),
        ),
        in_specs=[
            anywhere, anywhere, anywhere, anywhere, near, near, anywhere, near,
            pl.BlockSpec(memory_space=pltpu.SMEM),
        ],
        out_specs=(anywhere, anywhere, near),
        scratch_shapes=[
            pltpu.VMEM((MEM, features), short),
            pltpu.VMEM((rows, features), short),
            pltpu.VMEM((rows, features), short),
            pltpu.VMEM((features, key_width), short),
            pltpu.VMEM((features, part), short),
            pltpu.VMEM((features, width), short),
            pltpu.VMEM((4, width, key_width), short),
            pltpu.VMEM((mem_total, features), short),
            pltpu.VMEM((seg_count, mem_total, part), short),
            pltpu.VMEM((seg_count, mem_total, width), short),
            pltpu.VMEM((4 * rows, key_width), short),
            pltpu.VMEM((seg_count, rows, width), short),
            pltpu.VMEM((4, rows, width), short),
            pltpu.VMEM((6, rows, width), short),
            pltpu.VMEM((rows, features), short),
            pltpu.VMEM((width, key_width), short),
            pltpu.VMEM((rows, mem_total), short),
            dma((4,)), dma((3,)), dma((3,)), dma((3, 8)), dma((3, 8)),
            dma((9,)), dma((seg_count,)), dma((9,)), dma((seg_count,)),
            dma((9,)), dma((seg_count,)), dma((3, 2)), dma((3, 2)),
            dma((16,)), dma((seg_count, 2)), dma((1 + seg_count,)),
        ],
        compiler_params=pltpu.CompilerParams(
            collective_id=0, has_side_effects=True, vmem_limit_bytes=63 * 1024 * 1024
        ),
    )(
        leaving, w_query, w_key, w_value, w_gate, norm_gain, memory_matrix, key_totals, doc_starts
    )
    return (updated, matrix_next, totals_next)


def local(
    leaving, w_query, w_key, w_value, w_gate, norm_gain, memory_matrix, key_totals, doc_starts
):
    seg_count = lax.axis_size("seg")
    my_index = lax.axis_index("seg")
    memory_rows = shifted(leaving[0, 0, :MEM], "section", 1)
    entering = shifted(leaving, "section", 1)[0, 0]
    matrix = memory_matrix[0]
    whole_matrix = lax.all_gather(matrix, "seg", axis=0, tiled=True)
    memory = lax.all_gather(normalized(memory_rows, norm_gain[0]), "seg", axis=0, tiled=True)
    key_part = feature_map(jnp.dot(memory, w_key[0], preferred_element_type=jnp.float32)).astype(
        jnp.bfloat16
    )
    value_part = jnp.dot(memory, w_value[0], preferred_element_type=jnp.float32)
    gate_rates = jax.nn.sigmoid(jnp.dot(memory, w_gate[0], preferred_element_type=jnp.float32))
    key_rows = lax.all_gather(key_part, "seg", axis=1, tiled=True)
    fresh_flag, seen_pairs, seen_final = visibility(doc_starts[0])
    key_wide = key_rows.astype(jnp.float32)
    key_sums = key_wide.reshape(seg_count, MEM, -1).sum(axis=1)
    totals = fresh_flag[:, None] * key_totals[0][None, :] + jnp.dot(
        seen_pairs.T, key_sums, precision=highest
    )
    total_rows = jnp.repeat(totals, MEM, axis=0)
    key_scales = jnp.maximum(jnp.sum(total_rows * key_wide, axis=-1), 1.0)
    key_gram = contract_last(key_rows, key_rows)
    seen_cols = jnp.repeat(jnp.repeat(seen_pairs, MEM, axis=0), MEM, axis=1)
    mixing = seen_cols * key_gram * (gate_rates / key_scales)[None, :]
    fresh_rows = jnp.repeat(fresh_flag, MEM)
    probed_keys = contract_last(key_rows, matrix)
    initial = gate_rates[:, None] * (
        value_part - (fresh_rows / key_scales)[:, None] * probed_keys
    )
    write_cols = solved(mixing, initial)
    writes = lax.all_gather(write_cols.astype(jnp.bfloat16), "seg", axis=1, tiled=True)
    fresh_end = fresh_flag[seg_count - 1]
    end_rows = jnp.repeat(seen_final, MEM)
    matrix_next = (
        fresh_end * matrix.astype(jnp.float32)
        + contract_first(write_cols * end_rows[:, None], key_wide)
    ).astype(jnp.bfloat16)
    totals_next = fresh_end * key_totals[0] + jnp.dot(seen_final, key_sums, precision=highest)
    normed = normalized(entering, norm_gain[0])
    queries = feature_map(jnp.dot(normed, w_query[0], preferred_element_type=jnp.float32)).astype(
        jnp.bfloat16
    )
    my_fresh = fresh_flag[my_index]
    column_mask = jnp.repeat(seen_pairs[:, my_index], MEM)
    my_totals = lax.dynamic_slice_in_dim(totals, my_index, 1, 0)
    denominator = jnp.maximum(jnp.sum(queries.astype(jnp.float32) * my_totals, axis=-1), 1.0)
    similarity = contract_last(queries, key_rows) * column_mask[None, :]
    low_rank = jnp.dot(
        similarity.astype(jnp.bfloat16), writes, preferred_element_type=jnp.float32
    )
    base_read = contract_last(queries, whole_matrix)
    updated = (
        entering.astype(jnp.float32) + (my_fresh * base_read + low_rank) / denominator[:, None]
    ).astype(jnp.bfloat16)
    return (updated[None, None], matrix_next[None], totals_next[None])


def solution(mesh):
    fits = mesh.shape["seg"] == 8 and mesh.shape["section"] > 2
    return jax.shard_map(
        chained if fits else local,
        mesh=mesh,
        in_specs=(
            P("seg", "section", None, None),
            P("section", None, None),
            P("section", None, "seg"),
            P("section", None, "seg"),
            P("section", None),
            P("section", None),
            P("section", "seg", None),
            P("section", None),
            P("section", None),
        ),
        out_specs=(P("seg", "section", None, None), P("section", "seg", None), P("section", None)),
        check_vma=False,
    )
```

```python
import jax
import jax.numpy as jnp
from jax import lax
from jax.experimental import pallas as pl
from jax.experimental.pallas import tpu as pltpu
from jax.sharding import PartitionSpec as P

MEM = 16


highest = lax.Precision.HIGHEST
epsilon = 1e-05


def shifted(shard, axis, by):
    size = lax.axis_size(axis)
    return lax.ppermute(shard, axis, [(i, (i + by) % size) for i in range(size)])


def feature_map(projected):
    return jax.nn.elu(projected) + 1.0


def contract_last(left_rows, right_rows):
    return lax.dot_general(
        left_rows, right_rows, (((1,), (1,)), ((), ())), preferred_element_type=jnp.float32
    )


def contract_first(left_rows, right_rows):
    return lax.dot_general(
        left_rows,
        right_rows,
        (((0,), (0,)), ((), ())),
        precision=highest,
        preferred_element_type=jnp.float32,
    )


def visibility(starts_row):
    seg_total = starts_row.shape[0]
    positions = jnp.arange(seg_total, dtype=jnp.int32)
    last_start = lax.cummax(jnp.where(starts_row == 1, positions, jnp.int32(-1)), axis=0)
    fresh_flag = (last_start < 0).astype(jnp.float32)
    seen_pairs = (
        (positions[:, None] >= last_start[None, :]) & (positions[:, None] < positions[None, :])
    ).astype(jnp.float32)
    seen_final = (positions >= last_start[seg_total - 1]).astype(jnp.float32)
    return (fresh_flag, seen_pairs, seen_final)


def normalized(rows, gain_row):
    wide = rows.astype(jnp.float32)
    inverse_rms = lax.rsqrt(jnp.mean(wide * wide, axis=-1, keepdims=True) + epsilon)
    return (wide * inverse_rms * gain_row.astype(jnp.float32)).astype(jnp.bfloat16)


def solved(mixing, initial):
    size = mixing.shape[0]
    power = -mixing.T
    writes = initial + jnp.dot(power, initial, precision=highest)
    span = 2
    while span < size // MEM:
        power = jnp.dot(power, power, precision=highest)
        writes = writes + jnp.dot(power, writes, precision=highest)
        span *= 2
    return writes


def rows_by_rows(left, right, precision=None):
    return lax.dot_general(
        left,
        right,
        (((1,), (1,)), ((), ())),
        precision=precision,
        preferred_element_type=jnp.float32,
    )


def phi(v):
    return jnp.where(v > 0, v + 1.0, jnp.exp(jnp.minimum(v, 0.0)))


def chain_kernel(
    leaving, w_query, w_key, w_value, w_gate, gain, matrix, totals_in, starts,
    updated, matrix_out, totals_out,
    mem_rows, rows, normed, wq, wk, wv, slots, memory, keys, writes, queries, base, stage, guests,
    final, matrix_new, sims,
    load_sem, shift_send, shift_recv, slot_send, slot_recv, mem_send, mem_recv, key_send, key_recv,
    write_send, write_recv, query_send, query_recv, base_send, base_recv, store_sem,
):
    seg = lax.axis_index("seg")
    section = lax.axis_index("section")
    sections = lax.axis_size("section")
    z = seg // 2
    core = seg % 2
    pair = z + 1 - 2 * (z % 2)
    inner = (z + 1) // 2 == 1
    outer = (z + 1) // 2 != 1
    middle = jnp.where(inner, 3 - z, 3 - pair)
    far = jnp.where(inner, 3 - pair, 3 - z)
    partner = 2 * z + 1 - core
    pair_seg = 2 * pair + core
    pair_cross = 2 * pair + 1 - core
    across_seg = 2 * (3 - z) + core
    after = (section + 1) % sections
    before = (section + sections - 1) % sections
    row_count = rows.shape[0]
    width = slots.shape[1]
    part = keys.shape[2]
    seg_count = keys.shape[0]
    mem_total = memory.shape[0]
    half = width // 2
    pieces = slot_send.shape[1]
    depth = width // pieces

    def remote(src, dst, send, recv, to_seg, to_section=section):
        return pltpu.make_async_remote_copy(
            src_ref=src, dst_ref=dst, send_sem=send, recv_sem=recv,
            device_id=(to_seg, to_section), device_id_type=pl.DeviceIdType.MESH,
        )

    loads = [
        pltpu.make_async_copy(w_key.at[0], wk, load_sem.at[0]),
        pltpu.make_async_copy(w_value.at[0], wv, load_sem.at[1]),
        pltpu.make_async_copy(matrix.at[0], slots.at[0], load_sem.at[2]),
        pltpu.make_async_copy(w_query.at[0], wq, load_sem.at[3]),
    ]
    for load in loads:
        load.start()

    barrier = pltpu.get_barrier_semaphore()
    for to_seg, to_section in (
        (seg, after), (seg, before), (partner, section), (pair_seg, section), (pair_cross, section)
    ):
        pl.semaphore_signal(
            barrier, inc=1, device_id=(to_seg, to_section), device_id_type=pl.DeviceIdType.MESH
        )

    @pl.when(inner)
    def _():
        pl.semaphore_signal(
            barrier, inc=1, device_id=(across_seg, section), device_id_type=pl.DeviceIdType.MESH
        )
        pl.semaphore_wait(barrier, 6)

    @pl.when(outer)
    def _():
        pl.semaphore_wait(barrier, 5)

    mem_shift = remote(
        leaving.at[0, 0, pl.ds(0, MEM)], mem_rows, shift_send.at[0], shift_recv.at[0], seg, after
    )
    mem_shift.start()
    cut = (row_count // 2 + 15) // 16 * 16
    bounds = ((0, cut), (cut, row_count))
    row_shift = []
    for n, (low, high) in enumerate(bounds):
        some = pl.ds(low, high - low)
        row_shift.append(
            remote(
                leaving.at[0, 0, some], rows.at[some], shift_send.at[1 + n],
                shift_recv.at[1 + n], seg, after,
            )
        )
        row_shift[n].start()

    def slot_copy(kind, piece):
        span = pl.ds(piece * depth, depth)
        source = slots.at[1, span] if kind == 3 else matrix.at[0, span]
        to_seg = pair_seg if kind == 1 else across_seg
        return remote(
            source, slots.at[kind, span], slot_send.at[kind - 1, piece],
            slot_recv.at[kind - 1, piece], to_seg,
        )

    def pump(first, last):
        for number in range(first, last):
            if number < pieces:
                @pl.when(outer)
                def _():
                    slot_copy(1, number).start()

                @pl.when(inner)
                def _():
                    slot_copy(2, number).start()
            else:
                @pl.when(inner)
                def _():
                    slot_copy(1, number - pieces).wait_recv()
                    slot_copy(3, number - pieces).start()

    pump(0, 1)

    same_core = [2 * chip + core for chip in (pair, middle, far)]
    other_core = [2 * chip + 1 - core for chip in (z, pair, middle, far)]

    def gather(view, send, recv):
        def copy(index, number, to_seg):
            return remote(view(index), view(index), send.at[number], recv.at[index], to_seg)

        def begin():
            copy(seg, 0, pair_seg).start()

            @pl.when(inner)
            def _():
                copy(seg, 1, across_seg).start()

            copy(seg, 2, partner).start()

        def relay(k):
            index = same_core[k]
            copy(index, 3 + k, partner).wait_recv()

            @pl.when(inner)
            def _():
                copy(index, 6 + k, across_seg if k == 0 else pair_seg).start()

            copy(index, 3 + k, partner).start()

        def arrive():
            for index in other_core:
                copy(index, 0, partner).wait_recv()

        def finish():
            copy(seg, 0, pair_seg).wait_send()
            copy(seg, 2, partner).wait_send()
            for k, index in enumerate(same_core):
                copy(index, 3 + k, partner).wait_send()

            @pl.when(inner)
            def _():
                copy(seg, 1, across_seg).wait_send()
                for k, index in enumerate(same_core):
                    copy(index, 6 + k, pair_seg).wait_send()

        return begin, relay, arrive, finish

    gain_row = gain[...].astype(jnp.float32)

    def normalize(some):
        wide = some.astype(jnp.float32)
        scale = lax.rsqrt(jnp.mean(wide * wide, axis=-1, keepdims=True) + epsilon)
        return (wide * scale * gain_row).astype(jnp.bfloat16)

    mem_begin, mem_relay, mem_arrive, mem_finish = gather(
        lambda index: memory.at[pl.ds(pl.multiple_of(index * MEM, MEM), MEM)], mem_send, mem_recv
    )
    mem_shift.wait_recv()
    memory[pl.ds(pl.multiple_of(seg * MEM, MEM), MEM), :] = normalize(mem_rows[...])
    mem_begin()
    for k in range(3):
        pump(1 + k, 2 + k)
        mem_relay(k)
    pump(4, 5)
    mem_arrive()

    key_begin, key_relay, key_arrive, key_finish = gather(
        lambda index: keys.at[index], key_send, key_recv
    )
    loads[0].wait()
    keys[seg] = phi(
        jnp.dot(memory[...], wk[...], preferred_element_type=jnp.float32)
    ).astype(jnp.bfloat16)
    key_begin()
    pump(5, 6)
    loads[1].wait()
    values = jnp.dot(memory[...], wv[...], preferred_element_type=jnp.float32)
    gate_logits = jnp.sum(
        memory[...].astype(jnp.float32) * w_gate[...].astype(jnp.float32), axis=-1, keepdims=True
    )
    rates = 1.0 / (1.0 + jnp.exp(-gate_logits))
    def query_copy(kind, n):
        low, high = bounds[n]
        span = pl.ds((2 * row_count if kind == 2 else 0) + low, high - low)
        landing = pl.ds((1 + kind) * row_count + low, high - low)
        return remote(
            queries.at[span], queries.at[landing], query_send.at[kind, n],
            query_recv.at[kind, n], pair_seg if kind == 1 else partner,
        )

    def make_queries(n):
        low, high = bounds[n]
        row_shift[n].wait_recv()

        @pl.loop(low // 16, high // 16)
        def _(step):
            some = pl.ds(pl.multiple_of(step * 16, 16), 16)
            normed[some, :] = normalize(rows[some, :])

        if n == 0:
            loads[3].wait()

        @pl.loop(0, seg_count)
        def _(b):
            cols = pl.ds(pl.multiple_of(b * part, part), part)
            queries[low:high, cols] = phi(
                jnp.dot(normed[low:high, :], wq[:, cols], preferred_element_type=jnp.float32)
            ).astype(jnp.bfloat16)

        @pl.when(outer)
        def _():
            query_copy(1, n).start()

        query_copy(0, n).start()

    def pass_guests(n):
        @pl.when(inner)
        def _():
            query_copy(1, n).wait_recv()
            query_copy(2, n).start()

    for k in range(3):
        key_relay(k)
        pump(6 + k, 7 + k)
    key_arrive()
    pump(9, 11)

    def last_start(positions):
        last = jnp.full(positions.shape, -1, jnp.int32)
        for j in range(seg_count):
            last = jnp.maximum(last, jnp.where((starts[0, j] == 1) & (positions >= j), j, -1))
        return last

    square = (mem_total, mem_total)
    to_segment = lax.broadcasted_iota(jnp.int32, square, 0) // MEM
    from_segment = lax.broadcasted_iota(jnp.int32, square, 1) // MEM
    seen = ((from_segment >= last_start(to_segment)) & (from_segment < to_segment)).astype(
        jnp.float32
    )
    row_segment = lax.broadcasted_iota(jnp.int32, (mem_total, 1), 0) // MEM
    fresh_rows = (last_start(row_segment) < 0).astype(jnp.float32)
    final_segment = jnp.full((mem_total, 1), seg_count - 1, jnp.int32)
    end_last = last_start(final_segment)
    end_rows = (row_segment >= end_last).astype(jnp.float32)
    fresh_end = (end_last[:1] < 0).astype(jnp.float32)

    loads[2].wait()
    gram = jnp.zeros(square, jnp.float32)
    probed = jnp.zeros((mem_total, width), jnp.float32)
    start_scale = jnp.zeros((mem_total, 1), jnp.float32)
    for b in range(seg_count):
        cols = pl.ds(b * part, part)
        block = keys[b]
        gram += rows_by_rows(block, block)
        probed += rows_by_rows(block, slots[0, :, cols])
        start_scale += jnp.sum(
            block.astype(jnp.float32) * totals_in[:, cols], axis=-1, keepdims=True
        )
    visible = seen * gram
    scales = jnp.maximum(
        fresh_rows * start_scale + jnp.sum(visible, axis=-1, keepdims=True), 1.0
    )
    power = -(rates / scales) * visible
    solved_rows = rates * (values - (fresh_rows / scales) * probed)
    span = 1
    while span < seg_count:
        solved_rows += jnp.dot(
            power, solved_rows, precision=highest, preferred_element_type=jnp.float32
        )
        span *= 2
        if span < seg_count:
            power = jnp.dot(power, power, precision=highest, preferred_element_type=jnp.float32)
    write_begin, write_relay, write_arrive, write_finish = gather(
        lambda index: writes.at[index], write_send, write_recv
    )
    writes[seg] = solved_rows.astype(jnp.bfloat16)
    write_begin()

    pump(11, 12)
    make_queries(0)
    for k in range(3):
        write_relay(k)
        pump(12 + k, 13 + k)
    pump(15, 2 * pieces)
    make_queries(1)
    pass_guests(0)

    key_segment = lax.broadcasted_iota(jnp.int32, (1, mem_total), 1) // MEM
    my_segment = jnp.full((1, mem_total), 0, jnp.int32) + seg
    my_last = last_start(my_segment)
    my_mask = ((key_segment >= my_last) & (key_segment < my_segment)).astype(jnp.float32)
    my_fresh = (my_last[:, :1] < 0).astype(jnp.float32)
    similarity = jnp.zeros((row_count, mem_total), jnp.float32)
    query_scale = jnp.zeros((row_count, 1), jnp.float32)
    for b in range(seg_count):
        cols = pl.ds(b * part, part)
        mine = queries[:row_count, cols]
        similarity += rows_by_rows(mine, keys[b])
        query_scale += jnp.sum(
            mine.astype(jnp.float32) * totals_in[:, cols], axis=-1, keepdims=True
        )
    similarity *= my_mask
    inverse = 1.0 / jnp.maximum(
        my_fresh * query_scale + jnp.sum(similarity, axis=-1, keepdims=True), 1.0
    )
    sims[...] = similarity.astype(jnp.bfloat16)
    my_scale = my_fresh * inverse

    ended = (solved_rows * end_rows).T
    for b in range(seg_count):
        cols = pl.ds(b * part, part)
        block = keys[b].astype(jnp.float32)
        matrix_new[:, cols] = (
            fresh_end * slots[0, :, cols].astype(jnp.float32)
            + jnp.dot(ended, block, precision=highest, preferred_element_type=jnp.float32)
        ).astype(jnp.bfloat16)
        totals_out[:, cols] = fresh_end * totals_in[:, cols] + jnp.sum(
            end_rows * block, axis=0, keepdims=True
        )
    matrix_store = pltpu.make_async_copy(matrix_new, matrix_out.at[0], store_sem.at[0])
    matrix_store.start()

    def partner_copy(slot, column):
        return remote(
            stage.at[slot], base.at[column], base_send.at[slot], base_recv.at[column, 0], partner
        )

    def partner_half(h, column):
        cols = pl.ds(h * half, half)
        return remote(
            stage.at[3, :, cols], base.at[column, :, cols], base_send.at[10 + h],
            base_recv.at[column, h], partner,
        )

    guest_slots = (0, 2)

    def guest_copy(number, which, column):
        return remote(
            guests.at[2 * number + which], base.at[column], base_send.at[4 + 2 * number + which],
            base_recv.at[column, 0], pair_cross if which else pair_seg,
        )

    def guest_half(h, which, column):
        cols = pl.ds(h * half, half)
        return remote(
            guests.at[4 + which, :, cols], base.at[column, :, cols],
            base_send.at[12 + 2 * h + which], base_recv.at[column, h],
            pair_cross if which else pair_seg,
        )

    def far_read(h, column):
        cols = pl.ds(h * half, half)
        for piece in range(h * pieces // 2, (h + 1) * pieces // 2):
            slot_copy(3, piece).wait_recv()
        part_read = rows_by_rows(queries[...], slots[3, pl.ds(h * half, half)]).astype(
            jnp.bfloat16
        )
        for which in range(2):
            guests[4 + which, :, cols] = part_read[
                (2 + which) * row_count : (3 + which) * row_count
            ]
            guest_half(h, which, column).start()
        stage[3, :, cols] = part_read[row_count : 2 * row_count]
        partner_half(h, column).start()
        base[column, :, cols] = part_read[:row_count]

    def chip_read(slot, column):
        part_read = rows_by_rows(queries[: 2 * row_count], slots[slot]).astype(jnp.bfloat16)
        stage[slot] = part_read[row_count:]
        partner_copy(slot, column).start()
        base[column] = part_read[:row_count]

    def guest_read(number, column):
        part_read = rows_by_rows(
            queries[2 * row_count :], slots[guest_slots[number]]
        ).astype(jnp.bfloat16)
        for which in range(2):
            guests[2 * number + which] = part_read[which * row_count : (1 + which) * row_count]
            guest_copy(number, which, column).start()

    for n in range(2):
        query_copy(0, n).wait_recv()
    chip_read(0, seg)
    pass_guests(1)

    @pl.when(inner)
    def _():
        chip_read(1, same_core[0])
        for n in range(2):
            query_copy(2, n).wait_recv()
        guest_read(0, seg)
        for piece in range(pieces):
            slot_copy(2, piece).wait_recv()
        guest_read(1, same_core[1])
        chip_read(2, same_core[1])

    write_arrive()

    def combine(column):
        cols = pl.ds(pl.multiple_of(column * width, width), width)
        low = jnp.dot(sims[...], writes[column], preferred_element_type=jnp.float32)
        final[:, cols] = (
            rows[:, cols].astype(jnp.float32)
            + my_scale * base[column].astype(jnp.float32)
            + inverse * low
        ).astype(jnp.bfloat16)
        return pltpu.make_async_copy(
            final.at[:, cols], updated.at[0, 0, :, cols], store_sem.at[1 + column]
        )

    stores = [combine(seg)]
    stores[0].start()

    def landed(column, halves=False):
        if halves:
            partner_half(0, column).wait_recv()
            partner_half(1, column).wait_recv()
        else:
            partner_copy(0, column).wait_recv()

    landed(partner)
    stores.append(combine(partner))
    stores[-1].start()
    for k in range(3):
        if k == 2:
            @pl.when(inner)
            def _():
                far_read(0, same_core[2])
                far_read(1, same_core[2])

        @pl.when(outer)
        def _():
            landed(same_core[k], k == 2)

        stores.append(combine(same_core[k]))
        stores[-1].start()
        landed(other_core[k + 1], k == 2)
        stores.append(combine(other_core[k + 1]))
        stores[-1].start()

    mem_shift.wait_send()
    for n in range(2):
        row_shift[n].wait_send()
        query_copy(0, n).wait_send()
    partner_copy(0, seg).wait_send()

    @pl.when(outer)
    def _():
        for piece in range(pieces):
            slot_copy(1, piece).wait_send()
        for n in range(2):
            query_copy(1, n).wait_send()

    @pl.when(inner)
    def _():
        for piece in range(pieces):
            slot_copy(2, piece).wait_send()
            slot_copy(3, piece).wait_send()
        for n in range(2):
            query_copy(2, n).wait_send()
        for slot in (1, 2):
            partner_copy(slot, seg).wait_send()
        for which in range(2):
            for number in range(2):
                guest_copy(number, which, seg).wait_send()
            partner_half(which, seg).wait_send()
            for h in range(2):
                guest_half(h, which, seg).wait_send()

    mem_finish()
    key_finish()
    write_finish()
    matrix_store.wait()
    for store in stores:
        store.wait()


def chained(
    leaving, w_query, w_key, w_value, w_gate, norm_gain, memory_matrix, key_totals, doc_starts
):
    seg_count = lax.axis_size("seg")
    rows, features = leaving.shape[2:]
    key_width = w_query.shape[2]
    part = w_key.shape[2]
    width = memory_matrix.shape[1]
    mem_total = seg_count * MEM
    short = jnp.bfloat16
    anywhere = pl.BlockSpec(memory_space=pl.ANY)
    near = pl.BlockSpec(memory_space=pltpu.VMEM)
    dma = pltpu.SemaphoreType.DMA
    updated, matrix_next, totals_next = pl.pallas_call(
        chain_kernel,
        out_shape=(
            jax.ShapeDtypeStruct(leaving.shape, short),
            jax.ShapeDtypeStruct(memory_matrix.shape, short),
            jax.ShapeDtypeStruct(key_totals.shape, jnp.float32),
        ),
        in_specs=[
            anywhere, anywhere, anywhere, anywhere, near, near, anywhere, near,
            pl.BlockSpec(memory_space=pltpu.SMEM),
        ],
        out_specs=(anywhere, anywhere, near),
        scratch_shapes=[
            pltpu.VMEM((MEM, features), short),
            pltpu.VMEM((rows, features), short),
            pltpu.VMEM((rows, features), short),
            pltpu.VMEM((features, key_width), short),
            pltpu.VMEM((features, part), short),
            pltpu.VMEM((features, width), short),
            pltpu.VMEM((4, width, key_width), short),
            pltpu.VMEM((mem_total, features), short),
            pltpu.VMEM((seg_count, mem_total, part), short),
            pltpu.VMEM((seg_count, mem_total, width), short),
            pltpu.VMEM((4 * rows, key_width), short),
            pltpu.VMEM((seg_count, rows, width), short),
            pltpu.VMEM((4, rows, width), short),
            pltpu.VMEM((6, rows, width), short),
            pltpu.VMEM((rows, features), short),
            pltpu.VMEM((width, key_width), short),
            pltpu.VMEM((rows, mem_total), short),
            dma((4,)), dma((3,)), dma((3,)), dma((3, 8)), dma((3, 8)),
            dma((9,)), dma((seg_count,)), dma((9,)), dma((seg_count,)),
            dma((9,)), dma((seg_count,)), dma((3, 2)), dma((3, 2)),
            dma((16,)), dma((seg_count, 2)), dma((1 + seg_count,)),
        ],
        compiler_params=pltpu.CompilerParams(
            collective_id=0, has_side_effects=True, vmem_limit_bytes=63 * 1024 * 1024
        ),
    )(
        leaving, w_query, w_key, w_value, w_gate, norm_gain, memory_matrix, key_totals, doc_starts
    )
    return (updated, matrix_next, totals_next)


def local(
    leaving, w_query, w_key, w_value, w_gate, norm_gain, memory_matrix, key_totals, doc_starts
):
    seg_count = lax.axis_size("seg")
    my_index = lax.axis_index("seg")
    memory_rows = shifted(leaving[0, 0, :MEM], "section", 1)
    entering = shifted(leaving, "section", 1)[0, 0]
    matrix = memory_matrix[0]
    whole_matrix = lax.all_gather(matrix, "seg", axis=0, tiled=True)
    memory = lax.all_gather(normalized(memory_rows, norm_gain[0]), "seg", axis=0, tiled=True)
    key_part = feature_map(jnp.dot(memory, w_key[0], preferred_element_type=jnp.float32)).astype(
        jnp.bfloat16
    )
    value_part = jnp.dot(memory, w_value[0], preferred_element_type=jnp.float32)
    gate_rates = jax.nn.sigmoid(jnp.dot(memory, w_gate[0], preferred_element_type=jnp.float32))
    key_rows = lax.all_gather(key_part, "seg", axis=1, tiled=True)
    fresh_flag, seen_pairs, seen_final = visibility(doc_starts[0])
    key_wide = key_rows.astype(jnp.float32)
    key_sums = key_wide.reshape(seg_count, MEM, -1).sum(axis=1)
    totals = fresh_flag[:, None] * key_totals[0][None, :] + jnp.dot(
        seen_pairs.T, key_sums, precision=highest
    )
    total_rows = jnp.repeat(totals, MEM, axis=0)
    key_scales = jnp.maximum(jnp.sum(total_rows * key_wide, axis=-1), 1.0)
    key_gram = contract_last(key_rows, key_rows)
    seen_cols = jnp.repeat(jnp.repeat(seen_pairs, MEM, axis=0), MEM, axis=1)
    mixing = seen_cols * key_gram * (gate_rates / key_scales)[None, :]
    fresh_rows = jnp.repeat(fresh_flag, MEM)
    probed_keys = contract_last(key_rows, matrix)
    initial = gate_rates[:, None] * (
        value_part - (fresh_rows / key_scales)[:, None] * probed_keys
    )
    write_cols = solved(mixing, initial)
    writes = lax.all_gather(write_cols.astype(jnp.bfloat16), "seg", axis=1, tiled=True)
    fresh_end = fresh_flag[seg_count - 1]
    end_rows = jnp.repeat(seen_final, MEM)
    matrix_next = (
        fresh_end * matrix.astype(jnp.float32)
        + contract_first(write_cols * end_rows[:, None], key_wide)
    ).astype(jnp.bfloat16)
    totals_next = fresh_end * key_totals[0] + jnp.dot(seen_final, key_sums, precision=highest)
    normed = normalized(entering, norm_gain[0])
    queries = feature_map(jnp.dot(normed, w_query[0], preferred_element_type=jnp.float32)).astype(
        jnp.bfloat16
    )
    my_fresh = fresh_flag[my_index]
    column_mask = jnp.repeat(seen_pairs[:, my_index], MEM)
    my_totals = lax.dynamic_slice_in_dim(totals, my_index, 1, 0)
    denominator = jnp.maximum(jnp.sum(queries.astype(jnp.float32) * my_totals, axis=-1), 1.0)
    similarity = contract_last(queries, key_rows) * column_mask[None, :]
    low_rank = jnp.dot(
        similarity.astype(jnp.bfloat16), writes, preferred_element_type=jnp.float32
    )
    base_read = contract_last(queries, whole_matrix)
    updated = (
        entering.astype(jnp.float32) + (my_fresh * base_read + low_rank) / denominator[:, None]
    ).astype(jnp.bfloat16)
    return (updated[None, None], matrix_next[None], totals_next[None])


def solution(mesh):
    fits = mesh.shape["seg"] == 8 and mesh.shape["section"] > 2
    return jax.shard_map(
        chained if fits else local,
        mesh=mesh,
        in_specs=(
            P("seg", "section", None, None),
            P("section", None, None),
            P("section", None, "seg"),
            P("section", None, "seg"),
            P("section", None),
            P("section", None),
            P("section", "seg", None),
            P("section", None),
            P("section", None),
        ),
        out_specs=(P("seg", "section", None, None), P("section", "seg", None), P("section", None)),
        check_vma=False,
    )
```
